32 devices in a mesh: sp: 8 (over y, x, core), dp: 4 (over z).
Axes of the slice: x: 2, y: 2, z: 4, core: 2. Of those that a mesh axis runs over, the one named last changes fastest.
Arguments:
- tokens: bfloat16 [16, 1024, 1536], P('dp', 'sp'), may hold values from -6 to 6
- norm_gain: bfloat16 [1536], P('sp'), may hold values from 0.099609375 to 1.8984375
- in_weight: bfloat16 [1536, 6400], P('sp'), may hold values from -0.15625 to 0.15625
- step_weight: bfloat16 [1536, 48], P('sp'), may hold values from -0.15625 to 0.15625
- filter_weight: bfloat16 [4, 3328], P(None, 'sp'), may hold values from -3 to 3
- filter_bias: bfloat16 [3328], P('sp'), may hold values from -3 to 3
- step_bias: bfloat16 [48], P('sp'), may hold values from -5.5 to -3.5
- log_rate: bfloat16 [48], P('sp'), may hold values from -9 to 2
- skip_scale: bfloat16 [48], P('sp'), may hold values from 0.5 to 1.5
- inner_gain: bfloat16 [3072], P('sp'), may hold values from 0.099609375 to 1.8984375
- out_weight: bfloat16 [3072, 1536], P('sp'), may hold values from -0.109375 to 0.109375
- cotangent: bfloat16 [16, 1024, 1536], P('dp', 'sp'), may hold values from -6 to 6
Outputs:
- output: bfloat16 [16, 1024, 1536], P('dp', 'sp')
- token_gradient: float32 [16, 1024, 1536], P('dp', 'sp')
- norm_gain_gradient: float32 [1536], P('sp')
- in_gradient: float32 [1536, 6400], P('sp')
- step_gradient: float32 [1536, 48], P('sp')
- filter_gradient: float32 [4, 3328], P(None, 'sp')
- filter_bias_gradient: float32 [3328], P('sp')
- step_bias_gradient: float32 [48], P('sp')
- rate_gradient: float32 [48], P('sp')
- skip_gradient: float32 [48], P('sp')
- inner_gain_gradient: float32 [3072], P('sp')
- out_gradient: float32 [3072, 1536], P('sp')
The draws below stay inside these ranges and needn't reach their ends.
All inputs are finite; a program needn't handle non-finite values.
Results may differ from the reference program's by a relative error of at most 0.0076.
Values may be sent and summed in bfloat16 or wider, within the bound.
No kernel may reach another device: no remote copies, remote signals or barrier semaphores. Data moves between devices by JAX's collectives and lax.ppermute only.
A program may use at most 384 MiB of HBM per device.

```python
import jax
import jax.numpy as jnp
from jax import lax

D = 1536
H = 48
P_SIZE = 64
N = 128
K = 4
DI = 3072
CH = 3328
LENGTH = 1024
BATCH = 16


def draw_log_rate(key, part):
    key = jax.random.fold_in(key, 7)
    pick_key, slow_key, fast_key = jax.random.split(key, 3)
    share = 0.5
    chosen = jax.random.uniform(pick_key, (H,)) < share
    slow = jax.random.uniform(slow_key, (H,), minval=jnp.log(0.05 / LENGTH), maxval=jnp.log(1.5 / LENGTH))
    fast = jax.random.uniform(fast_key, (H,), minval=jnp.log(0.02), maxval=jnp.log(0.05))
    return (jnp.where(chosen, slow, fast) - jnp.log(0.018)).astype(jnp.bfloat16)


def shard_levels(stream_key, dims, cuts, smallest, high):
    def one(dim, shards_of):
        draws = jax.random.uniform(jax.random.fold_in(jax.random.fold_in(stream_key, 6), dim), (shards_of,), jnp.float32, smallest / len(cuts), high / len(cuts))
        return jnp.repeat(jnp.exp(draws), dims[dim] // shards_of).reshape((-1,) + (1,) * (len(dims) - dim - 1))

    factor_of = one(*cuts[0])
    for cut in cuts[1:]:
        factor_of = factor_of * one(*cut)
    return factor_of


def bell_draw(stream_key, shape, scale, bound, shards=(), kind=jnp.bfloat16):
    values = scale * jax.random.normal(stream_key, shape, jnp.float32)
    if shards:
        values = values * shard_levels(stream_key, shape, shards, -0.22, 0.18)
    return jnp.clip(values, -bound, bound).astype(kind)


def setup_inputs(seed: int = 0) -> dict:
    streams_of = jax.random.split(jax.random.key(seed), 13)
    tokens = bell_draw(streams_of[0], (BATCH, LENGTH, D), 1.0, 6.0, ((0, 4), (1, 8)))
    norm_gain = jnp.clip(1.0 + 0.18 * jax.random.normal(streams_of[1], (D,), jnp.float32), 0.099609375, 1.8984375).astype(jnp.bfloat16)
    in_weight = bell_draw(streams_of[2], (D, 2 * DI + 2 * N), D ** -0.5, 0.15625, ((0, 8),))
    step_weight = bell_draw(streams_of[3], (D, H), D ** -0.5, 0.15625, ((0, 8),))
    filter_weight = bell_draw(streams_of[4], (K, CH), K ** -0.5, 3.0, ((1, 8),))
    filter_bias = bell_draw(streams_of[5], (CH,), 0.5, 3.0, ((0, 8),))
    step_bias = jnp.clip(-5.5 + 2.0 * jax.random.uniform(streams_of[6], (H,), jnp.float32) ** shard_levels(streams_of[6], (H,), ((0, 8),), -0.2, 0.2), -5.5, -3.5).astype(jnp.bfloat16)
    log_rate = draw_log_rate(jax.random.fold_in(streams_of[12], 71), 0)
    skip_scale = jnp.clip(0.5 + 1.0 * jax.random.uniform(streams_of[8], (H,), jnp.float32) ** shard_levels(streams_of[8], (H,), ((0, 8),), -0.2, 0.2), 0.5, 1.5).astype(jnp.bfloat16)
    inner_gain = jnp.clip(1.0 + 0.18 * jax.random.normal(streams_of[9], (DI,), jnp.float32), 0.099609375, 1.8984375).astype(jnp.bfloat16)
    out_weight = bell_draw(streams_of[10], (DI, D), DI ** -0.5, 0.109375, ((0, 8),))
    cotangent = bell_draw(streams_of[11], (BATCH, LENGTH, D), 1.0, 6.0, ((0, 4), (1, 8)))
    return {"tokens": tokens, "norm_gain": norm_gain, "in_weight": in_weight, "step_weight": step_weight, "filter_weight": filter_weight, "filter_bias": filter_bias, "step_bias": step_bias, "log_rate": log_rate, "skip_scale": skip_scale, "inner_gain": inner_gain, "out_weight": out_weight, "cotangent": cotangent}


EPSILON = 1e-05
precise = lax.Precision.HIGHEST

@jax.custom_vjp
def low(v):
    return lax.optimization_barrier(v.astype(jnp.bfloat16)).astype(jnp.float32)

@jax.custom_vjp
def low_back(v):
    return v

def low_keep(v):
    return (low(v), None)

def low_pass(kept, grad):
    return (grad,)

def back_keep(v):
    return (v, None)

def back_low(kept, grad):
    return (low(grad),)
low.defvjp(low_keep, low_pass)
low_back.defvjp(back_keep, back_low)

def scale_rows(value_rows, gain):
    return value_rows * lax.rsqrt(lax.optimization_barrier(jnp.mean(value_rows * value_rows, axis=-1, keepdims=True)) + EPSILON) * gain

def block_out(signal, steps, entry, readout, rate, skip_scale, state):
    running = jnp.cumsum(steps * rate, axis=0)
    width = signal.shape[0]
    rows = lax.broadcasted_iota(jnp.int32, (width, width), 0)
    cols = lax.broadcasted_iota(jnp.int32, (width, width), 1)
    below = (cols <= rows)[:, :, None]
    spans = jnp.where(below, running[:, None, :] - running[None, :, :], -1e+30)
    kernel = jnp.exp(spans)
    intersection = jnp.dot(readout, entry.T, precision=precise)
    mixing = kernel * intersection[:, :, None] * steps[None, :, :]
    result = jnp.einsum('tsh,shp->thp', mixing, signal, precision=precise)
    carried = jnp.einsum('tn,hpn->thp', readout, state, precision=precise)
    result = result + jnp.exp(running)[:, :, None] * carried + skip_scale[None, :, None] * signal
    remaining = jnp.exp(running[-1:, :] - running) * steps
    updated = jnp.exp(running[-1, :])[:, None, None] * state
    updated = updated + jnp.einsum('sh,shp,sn->hpn', remaining, signal, entry, precision=precise)
    return (result, updated)

def run_blocks(signal, steps, entry, readout, rate, skip_scale, state, width):
    length, heads, size = signal.shape
    count = length // width
    items = (signal.reshape(count, width, heads, size), steps.reshape(count, width, heads), entry.reshape(count, width, entry.shape[1]), readout.reshape(count, width, readout.shape[1]))

    def advance(carry, block):
        result, updated = block_out(block[0], block[1], block[2], block[3], rate, skip_scale, carry)
        return (updated, result)
    final, results = lax.scan(jax.checkpoint(advance), state, items)
    return (results.reshape(length, heads, size), final)

def layer(sequence, norm_gain, in_weight, step_weight, filter_weight, filter_bias, step_bias, log_rate, skip_scale, inner_gain, out_weight):
    length = sequence.shape[0]
    normed = low(scale_rows(sequence, norm_gain))
    projected_rows = low_back(jnp.dot(normed, in_weight, precision=precise))
    raw_steps = low_back(jnp.dot(normed, step_weight, precision=precise))
    gate = projected_rows[:, :DI]
    mixed_in = projected_rows[:, DI:]
    padded = jnp.concatenate([jnp.zeros((K - 1, CH), jnp.float32), mixed_in], axis=0)
    filtered = filter_bias
    for tap in range(K):
        filtered = filtered + filter_weight[tap] * padded[tap:tap + length]
    active = jax.nn.silu(filtered)
    signal = active[:, :DI].reshape(length, H, P_SIZE)
    entry = active[:, DI:DI + N]
    readout = active[:, DI + N:]
    steps = jax.nn.softplus(raw_steps + step_bias)
    rate = -jnp.exp(log_rate)
    result, _ = run_blocks(signal, steps, entry, readout, rate, skip_scale, jnp.zeros((H, P_SIZE, N), jnp.float32), min(length, 256))
    gated = result.reshape(length, DI) * jax.nn.silu(gate)
    mixed_out = low(scale_rows(gated, inner_gain))
    return sequence + jnp.dot(mixed_out, out_weight, precision=precise)

def reference(tokens, norm_gain, in_weight, step_weight, filter_weight, filter_bias, step_bias, log_rate, skip_scale, inner_gain, out_weight, cotangent):
    params = (norm_gain.astype(jnp.float32), in_weight.astype(jnp.float32), step_weight.astype(jnp.float32), filter_weight.astype(jnp.float32), filter_bias.astype(jnp.float32), step_bias.astype(jnp.float32), log_rate.astype(jnp.float32), skip_scale.astype(jnp.float32), inner_gain.astype(jnp.float32), out_weight.astype(jnp.float32))

    def one(totals, pair):
        sequence, backward_in = pair
        output, pull = jax.vjp(layer, sequence.astype(jnp.float32), *params)
        gradients = pull(backward_in.astype(jnp.float32))
        totals = tuple((total + gradient for total, gradient in zip(totals, gradients[1:])))
        return (totals, (output.astype(jnp.bfloat16), gradients[0]))
    start = tuple((jnp.zeros_like(param) for param in params))
    totals, (outputs, token_grads) = lax.scan(one, start, (tokens, cotangent))
    return (outputs, token_grads, totals[0], totals[1], totals[2], totals[3], totals[4], totals[5], totals[6], totals[7], totals[8], totals[9])
```

```python
import jax
import jax.numpy as jnp
from jax import lax
from jax.experimental import pallas as pl
from jax.experimental.pallas import tpu as pltpu
from jax.sharding import Mesh, PartitionSpec as P

N = 128
HEAD = 64
LANES = 128
VMEM = 60 * 1024 * 1024
EPSILON = 1e-05
f32, bf16 = jnp.float32, jnp.bfloat16
precise = lax.Precision.HIGHEST


def sigmoid(v):
    return 0.5 * jnp.tanh(0.5 * v) + 0.5


def dot(a, b):
    return jnp.dot(a, b, preferred_element_type=f32)


def dot_nt(a, b):
    return lax.dot_general(a, b, (((1,), (1,)), ((), ())), preferred_element_type=f32)


def spread_pair(low, a, p):
    return jnp.where(low, a[:, 2 * p : 2 * p + 1], a[:, 2 * p + 1 : 2 * p + 2])


def stacked(low, a):
    zero = jnp.zeros_like(a)
    return jnp.concatenate([jnp.where(low, a, zero), jnp.where(low, zero, a)], axis=0).astype(bf16)


def running_sum(x):
    rows = lax.broadcasted_iota(jnp.int32, x.shape, 0)
    k = 1
    while k < x.shape[0]:
        x = x + jnp.where(rows >= k, pltpu.roll(x, k, 0), 0.0)
        k *= 2
    return x


def forward_kernel(
    rank, projected, by_channel, by_head, result, scaled, squares, states, state, window
):
    step = pl.program_id(0)
    width, local = result.shape
    channels = local + 2 * N
    taps = 4

    @pl.when(step == 0)
    def _():
        state[...] = jnp.zeros_like(state)
        window[0:8, :] = jnp.zeros((8, channels), f32)

    @pl.when(step > 0)
    def _():
        window[0:8, :] = window[width : width + 8, :]

    window[8 : 8 + width, :] = projected[:, local : local + channels]
    filtered = by_channel[4:5, :]
    for tap in range(taps):
        at = 9 - taps + tap
        filtered = filtered + by_channel[tap : tap + 1, :] * window[at : at + width, :]
    active = filtered * sigmoid(filtered)
    entry = active[:, local : local + N]
    readout = active[:, local + N :].astype(bf16)
    steps = jax.nn.softplus(projected[:, local + channels :] + by_head[0:1, :])
    rows = lax.broadcasted_iota(jnp.int32, (width, width), 0)
    cols = lax.broadcasted_iota(jnp.int32, (width, width), 1)
    running = running_sum(steps * by_head[1:2, :])
    across = running.T
    meeting = jnp.where(cols <= rows, dot_nt(readout, entry.astype(bf16)), 0.0)
    before = state[...].astype(bf16)
    states[0] = before
    carried = dot(readout, before)
    entry_t = entry.T.astype(bf16)
    low = lax.broadcasted_iota(jnp.int32, (width, LANES), 1) < HEAD
    total = jnp.zeros((width, LANES), f32)
    weighted, decay = [], []
    for p in range(local // LANES):
        at = slice(p * LANES, (p + 1) * LANES)
        signal = active[:, at]
        mixing, along = [], []
        for h in (2 * p, 2 * p + 1):
            along.append(jnp.broadcast_to(running[:, h : h + 1], (width, width)))
            span = jnp.minimum(along[-1] - across[h : h + 1, :], 0.0)
            mixing.append((jnp.exp(span) * meeting).astype(bf16))
        entered = signal * spread_pair(low, steps, p)
        y = dot(jnp.concatenate(mixing, axis=1), stacked(low, entered))
        along = jnp.where(low, along[0], along[1])
        grown_p = jnp.exp(along)
        y = y + grown_p * carried[:, at] + by_channel[6:7, at] * signal
        result[:, at] = y
        gate = projected[:, at]
        gated = y * gate * sigmoid(gate)
        scaled[:, at] = (gated * by_channel[5:6, at]).astype(bf16)
        total = total + gated * gated
        weighted.append((entered * jnp.exp(along[width - 1 : width, :] - along)).astype(bf16))
        decay.append(grown_p[width - 1 : width, :])
    squares[...] = jnp.sum(total, axis=1, keepdims=True)
    state[...] = jnp.concatenate(decay, axis=1) * state[...] + dot(
        entry_t, jnp.concatenate(weighted, axis=1)
    )


def backward_kernel(
    rank,
    projected,
    tail,
    g_result,
    g_gate,
    states,
    by_channel,
    by_head,
    g_projected,
    sum_channel,
    sum_head,
    adjoint,
    window,
    ahead,
):
    step = pl.program_id(0)
    last = pl.num_programs(0) - 1
    width, local = g_result.shape
    channels = local + 2 * N
    taps = 4

    @pl.when(step == 0)
    def _():
        adjoint[...] = jnp.zeros_like(adjoint)
        ahead[width : width + 8, :] = jnp.zeros((8, channels), f32)
        sum_channel[...] = jnp.zeros_like(sum_channel)
        sum_head[...] = jnp.zeros_like(sum_head)

    @pl.when(step > 0)
    def _():
        ahead[width : width + 8, :] = ahead[0:8, :]

    window[0:8, :] = jnp.where(step == last, 0.0, tail[:, local : local + channels])
    window[8 : 8 + width, :] = projected[:, local : local + channels]
    filtered = by_channel[4:5, :]
    for tap in range(taps):
        at = 9 - taps + tap
        filtered = filtered + by_channel[tap : tap + 1, :] * window[at : at + width, :]
    gate_f = sigmoid(filtered)
    active = filtered * gate_f
    slope = gate_f * (1.0 + filtered * (1.0 - gate_f))
    entry = active[:, local : local + N]
    readout = active[:, local + N :]
    entry_b, readout_b = entry.astype(bf16), readout.astype(bf16)
    shifted = projected[:, local + channels :] + by_head[0:1, :]
    steps = jax.nn.softplus(shifted)
    rate = by_head[1:2, :]
    rows = lax.broadcasted_iota(jnp.int32, (width, width), 0)
    cols = lax.broadcasted_iota(jnp.int32, (width, width), 1)
    falls = steps * rate
    running = running_sum(falls)
    across = running.T
    meeting = jnp.where(rows <= cols, dot_nt(entry_b, readout_b), 0.0)
    before = states[0]
    after = adjoint[...].astype(bf16)
    carried = dot(readout_b, before)
    returned = dot(entry_b, after)
    readout_t = readout.T.astype(bf16)
    lane = lax.broadcasted_iota(jnp.int32, (width, LANES), 1)
    low = lane < HEAD
    g_projected[:, 0:local] = g_gate[...]
    ones = jnp.ones((width, LANES), bf16)
    by_col = jnp.zeros((width, LANES), f32)
    pick_rows = lax.broadcasted_iota(jnp.int32, (LANES, LANES), 0) // HEAD
    pick_cols = lax.broadcasted_iota(jnp.int32, (LANES, LANES), 1)
    g_meeting = jnp.zeros((width, width), f32)
    by_row = []
    per_head = jnp.zeros((3 * width + 8, LANES), f32)
    g_entry = jnp.zeros((width, N), f32)
    g_readout = jnp.zeros((width, N), f32)
    for p in range(local // LANES):
        at = slice(p * LANES, (p + 1) * LANES)
        signal = active[:, at]
        g_y = g_result[:, at].astype(f32)
        steps_p = spread_pair(low, steps, p)
        entered = signal * steps_p
        g_mixing = dot_nt(stacked(low, entered), g_result[:, at])
        mixing, along, parts = [], [], []
        for k, h in enumerate((2 * p, 2 * p + 1)):
            along.append(jnp.broadcast_to(running[:, h : h + 1], (width, width)))
            span = jnp.minimum(across[h : h + 1, :] - along[-1], 0.0)
            kernel = jnp.exp(span)
            mixing.append((kernel * meeting).astype(bf16))
            part = g_mixing[k * width : (k + 1) * width, :] * kernel
            g_meeting = g_meeting + part
            parts.append((part * meeting).astype(bf16))
            by_row.append(jnp.sum(parts[-1].astype(f32), axis=0, keepdims=True))
        across_sum = dot(jnp.concatenate(parts, axis=0), ones)
        for k, h in enumerate((2 * p, 2 * p + 1)):
            by_col = jnp.where(lane == h, across_sum[k * width : (k + 1) * width], by_col)
        along = jnp.where(low, along[0], along[1])
        grown_p = jnp.exp(along)
        left_p = jnp.exp(along[width - 1 : width, :] - along)
        back = left_p * returned[:, at]
        through = dot(jnp.concatenate(mixing, axis=1), stacked(low, g_y)) + back
        skip = by_channel[6:7, at]
        ahead[0:width, at] = steps_p * through + skip * g_y
        sum_channel[5:6, at] += jnp.sum(g_y * signal, axis=0, keepdims=True)
        g_grown = grown_p * g_y
        g_grown_b = g_grown.astype(bf16)
        before_p = before[:, at]
        after_p = adjoint[:, at]
        held = jnp.sum(after_p * before_p.astype(f32), axis=0, keepdims=True)
        pieces = jnp.concatenate(
            [
                signal * through,
                entered * back,
                g_grown * carried[:, at],
                jnp.broadcast_to(held, (8, LANES)),
            ],
            axis=0,
        )
        pick = jnp.where(pick_rows + 2 * p == pick_cols, 1.0, 0.0)
        per_head = per_head + dot(pieces.astype(bf16), pick.astype(bf16))
        g_readout = g_readout + dot_nt(g_grown_b, before_p)
        g_entry = g_entry + dot_nt((left_p * entered).astype(bf16), after[:, at])
        adjoint[:, at] = grown_p[width - 1 : width, :] * after_p + dot(readout_t, g_grown_b)
    g_meeting = jnp.where(rows <= cols, g_meeting, 0.0)
    g_readout = g_readout + dot(g_meeting.T.astype(bf16), entry_b)
    g_entry = g_entry + dot(g_meeting.astype(bf16), readout_b)
    heads = len(by_row)
    by_row = jnp.concatenate(by_row + [jnp.zeros((LANES - heads, width), f32)], axis=0).T
    direct = per_head[0:width]
    entering = per_head[width : 2 * width]
    rising = by_row + per_head[2 * width : 3 * width] - by_col
    change = entering - rising
    g_falls = (
        running_sum(change)
        - change
        + jnp.sum(rising, axis=0, keepdims=True)
        + jnp.exp(running[width - 1 : width, :]) * per_head[3 * width : 3 * width + 1]
    )
    g_steps = rate * g_falls + direct
    g_raw = g_steps * sigmoid(shifted)
    sum_head[0:1, :] += jnp.sum(g_raw, axis=0, keepdims=True)
    sum_head[1:2, :] += jnp.sum(falls * g_falls, axis=0, keepdims=True)
    g_projected[:, local + channels :] = g_raw.astype(bf16)
    ahead[0:width, local : local + N] = g_entry
    ahead[0:width, local + N :] = g_readout
    g_filtered = ahead[0:width, :] * slope
    ahead[0:width, :] = g_filtered
    g_in = jnp.zeros((width, channels), f32)
    for tap in range(taps):
        back_at = taps - 1 - tap
        g_in = g_in + by_channel[tap : tap + 1, :] * ahead[back_at : back_at + width, :]
        at = 9 - taps + tap
        sum_channel[tap : tap + 1, :] += jnp.sum(
            g_filtered * window[at : at + width, :], axis=0, keepdims=True
        )
    sum_channel[4:5, :] += jnp.sum(g_filtered, axis=0, keepdims=True)
    g_projected[:, local : local + channels] = g_in.astype(bf16)


def reversed_bits(chip, count):
    bits = count.bit_length() - 1
    return sum(((chip >> k) & 1) << (bits - 1 - k) for k in range(bits))


def slot_of(place, rank, pieces):
    count = pieces // 2
    half = count // 2
    core = (place ^ rank) & 1
    chip = (place ^ rank) >> 1
    at = jnp.where(core == 0, chip, reversed_bits(chip, count))
    return jnp.where(at < half, count, -half) + core * half + at


def chip_order(turn, count):
    return [j if turn == 0 else reversed_bits(j, count) for j in range(count)]


def slot_order(count):
    half = count // 2
    orders = [chip_order(turn, count) for turn in range(2)]
    return [
        (turn, orders[turn][upper * half + low])
        for upper in (1, 0)
        for turn in range(2)
        for low in range(half)
    ]


def scan_forward(rank, projected, by_channel, by_head, local, width):
    length, columns = projected.shape
    count = length // width
    channels = local + 2 * N

    def here(i, rank):
        return (slot_of(i, rank[0], count), 0)

    def fixed(i, rank):
        return (0, 0)

    return pl.pallas_call(
        forward_kernel,
        grid_spec=pltpu.PrefetchScalarGridSpec(
            num_scalar_prefetch=1,
            grid=(count,),
            in_specs=[
                pl.BlockSpec((width, columns), here),
                pl.BlockSpec((8, channels), fixed),
                pl.BlockSpec((8, LANES), fixed),
            ],
            out_specs=[
                pl.BlockSpec((width, local), here),
                pl.BlockSpec((width, local), here),
                pl.BlockSpec((width, 1), here),
                pl.BlockSpec((1, N, local), lambda i, rank: (i, 0, 0)),
            ],
            scratch_shapes=[
                pltpu.VMEM((N, local), f32),
                pltpu.VMEM((width + 8, channels), f32),
            ],
        ),
        out_shape=[
            jax.ShapeDtypeStruct((length, local), f32),
            jax.ShapeDtypeStruct((length, local), bf16),
            jax.ShapeDtypeStruct((length, 1), f32),
            jax.ShapeDtypeStruct((count, N, local), bf16),
        ],
        compiler_params=pltpu.CompilerParams(vmem_limit_bytes=VMEM),
        cost_estimate=pl.CostEstimate(flops=1_000_000, bytes_accessed=1_000_000, transcendentals=0),
        name="scan_forward",
    )(rank, projected, by_channel, by_head)


def scan_backward(rank, projected, g_result, g_gate, states, by_channel, by_head, width):
    length, columns = projected.shape
    local = g_result.shape[1]
    count = length // width
    channels = local + 2 * N

    def here(i, rank):
        return (slot_of(count - 1 - i, rank[0], count), 0)

    def tail(i, rank):
        earlier = jnp.maximum(count - 2 - i, 0)
        return (slot_of(earlier, rank[0], count) * (width // 8) + (width // 8 - 1), 0)

    def fixed(i, rank):
        return (0, 0)

    return pl.pallas_call(
        backward_kernel,
        grid_spec=pltpu.PrefetchScalarGridSpec(
            num_scalar_prefetch=1,
            grid=(count,),
            in_specs=[
                pl.BlockSpec((width, columns), here),
                pl.BlockSpec((8, columns), tail),
                pl.BlockSpec((width, local), here),
                pl.BlockSpec((width, local), here),
                pl.BlockSpec((1, N, local), lambda i, rank: (count - 1 - i, 0, 0)),
                pl.BlockSpec((8, channels), fixed),
                pl.BlockSpec((8, LANES), fixed),
            ],
            out_specs=[
                pl.BlockSpec((width, columns), here),
                pl.BlockSpec((8, channels), fixed),
                pl.BlockSpec((8, LANES), fixed),
            ],
            scratch_shapes=[
                pltpu.VMEM((N, local), f32),
                pltpu.VMEM((width + 8, channels), f32),
                pltpu.VMEM((width + 8, channels), f32),
            ],
        ),
        out_shape=[
            jax.ShapeDtypeStruct((length, columns), bf16),
            jax.ShapeDtypeStruct((8, channels), f32),
            jax.ShapeDtypeStruct((8, LANES), f32),
        ],
        compiler_params=pltpu.CompilerParams(vmem_limit_bytes=VMEM),
        cost_estimate=pl.CostEstimate(flops=1_000_000, bytes_accessed=1_000_000, transcendentals=0),
        name="scan_backward",
    )(rank, projected, projected, g_result, g_gate, states, by_channel, by_head)


BELOW = 16


def pack_kernel(
    place,
    in_weight,
    step_weight,
    filter_weight,
    filter_bias,
    inner_gain,
    norm_gain,
    per_head,
    *refs,
):
    parts, spread = refs[:-1], refs[-1]
    chips = len(parts)
    rows, columns = in_weight.shape[0], parts[0].shape[1]
    heads = step_weight.shape[1]
    local = (columns - 2 * N - LANES) // 2
    inner = local * chips
    channels = local + 2 * N
    each = heads // chips
    chip, core = place[0], place[1]
    taps, mine = filter_weight.shape
    at_row = lax.broadcasted_iota(jnp.int32, (heads, LANES), 0)
    at_lane = lax.broadcasted_iota(jnp.int32, (heads, LANES), 1)

    def laid(a, width, at):
        a = jnp.pad(a.astype(f32), ((0, 0), (0, width - a.shape[1])))
        return pltpu.roll(a, at, 1)

    filters = jnp.concatenate(
        [
            filter_weight[...].astype(f32),
            filter_bias[...].astype(f32),
            jnp.zeros((8 - taps - 1, mine), f32),
        ],
        axis=0,
    )
    spread[...] = laid(filters, spread.shape[1], (2 * chip + core) * mine)
    gain = laid(norm_gain[...], -(-chips * rows // LANES) * LANES, chip * rows)
    inner_row = laid(inner_gain[...], local, core * inner_gain.shape[1])
    head_rows = laid(per_head[...], LANES, core * (each // 2))
    for j in range(chips):
        c = chip ^ j
        out = parts[j]
        at = pl.ds(0, rows)
        from_gate = pl.ds(pl.multiple_of(c * local, LANES), local)
        out[at, 0:local] = in_weight[:, from_gate]
        out[at, local : 2 * local] = in_weight[
            :, pl.ds(pl.multiple_of(inner + c * local, LANES), local)
        ]
        out[at, 2 * local : 2 * local + 2 * N] = in_weight[:, 2 * inner :]
        pick = jnp.logical_and(at_row == c * each + at_lane, at_lane < each)
        pick = jnp.where(pick, 1.0, 0.0).astype(bf16)
        out[at, 2 * local + 2 * N :] = dot(step_weight[...], pick).astype(bf16)
        top = jnp.concatenate([spread[:, from_gate], spread[:, inner:]], axis=1)
        if j == 0:
            row = lax.broadcasted_iota(jnp.int32, (8, channels), 0)
            wide = jnp.pad(inner_row, ((0, 0), (0, 2 * N)))
            top = jnp.where(row == 5, wide, top)
        low = [jnp.zeros((8, LANES), f32) if j else head_rows, jnp.broadcast_to(gain, (8, gain.shape[1]))]
        low = jnp.concatenate(low, axis=1)
        low = jnp.pad(low, ((0, 0), (0, columns - low.shape[1])))
        top = jnp.pad(top, ((0, 0), (0, columns - channels)))
        out[rows:, :] = jnp.concatenate([top, low], axis=0).astype(bf16)


def pack_columns(place, arrays, per_head, chips, columns, inner):
    rows = arrays[0].shape[0] + BELOW
    vmem = pl.BlockSpec(memory_space=pltpu.VMEM)
    return pl.pallas_call(
        pack_kernel,
        in_specs=[pl.BlockSpec(memory_space=pltpu.SMEM)] + [vmem] * (len(arrays) + 1),
        out_specs=[vmem] * chips,
        out_shape=[jax.ShapeDtypeStruct((rows, columns), bf16)] * chips,
        scratch_shapes=[pltpu.VMEM((8, inner + 2 * N), f32)],
        compiler_params=pltpu.CompilerParams(vmem_limit_bytes=VMEM),
        cost_estimate=pl.CostEstimate(flops=1_000_000, bytes_accessed=1_000_000, transcendentals=0),
        name="pack_columns",
    )(place, *arrays, per_head)


def parameter_kernel(side, *refs):
    parts, (by_channel, by_head, gain) = refs[:-3], refs[-3:]
    channels = by_channel.shape[1]
    half = len(parts) // 2
    sums = [
        sum((part[...].astype(f32) for part in parts[k * half + 1 : (k + 1) * half]), parts[k * half][...].astype(f32))
        for k in range(2)
    ]
    whole = sums[0] + sums[1]
    heads = whole[8:16, 0:LANES]
    head = lax.broadcasted_iota(jnp.int32, (LANES, channels), 0)
    lane = lax.broadcasted_iota(jnp.int32, (LANES, channels), 1)
    expand = jnp.where(head == lane // HEAD, 1.0, 0.0).astype(bf16)
    skip = dot(heads[2:3].astype(bf16), expand)
    row = lax.broadcasted_iota(jnp.int32, (8, channels), 0)
    by_channel[...] = jnp.where(row == 6, skip, whole[0:8, 0:channels])
    row = lax.broadcasted_iota(jnp.int32, (8, LANES), 0)
    by_head[...] = jnp.where(
        row == 0, heads, jnp.where(row == 1, -jnp.exp(heads), 0.0)
    )
    gain[:, 0:side] = sums[0][8:9, LANES : LANES + side]
    gain[:, side:] = sums[1][8:9, LANES : LANES + side]


def parameters(parts, channels, width):
    total, columns = parts[0].shape
    at = total // BELOW - 1

    def whole(shape):
        return pl.BlockSpec(shape, lambda i: (0, 0))

    shapes = [(8, channels), (8, LANES), (1, width)]
    return pl.pallas_call(
        lambda *refs: parameter_kernel(width // 2, *refs),
        grid=(1,),
        in_specs=[pl.BlockSpec((BELOW, columns), lambda i: (at, 0))] * len(parts),
        out_specs=[whole(shape) for shape in shapes],
        out_shape=[jax.ShapeDtypeStruct(shape, f32) for shape in shapes],
        compiler_params=pltpu.CompilerParams(vmem_limit_bytes=VMEM),
        cost_estimate=pl.CostEstimate(flops=1_000_000, bytes_accessed=1_000_000, transcendentals=0),
        name="parameters",
    )(*parts)


def assemble_kernel(place, *refs):
    parts, out = refs[:-1], refs[-1]
    chips = len(parts) // 2
    rows = parts[0].shape[0] - BELOW
    for k in range(2):
        for j in range(chips):
            at = pl.multiple_of((k * chips + (place[0] ^ j)) * rows, BELOW)
            out[pl.ds(at, rows), :] = parts[k * chips + j][0:rows, :]


def assembled(place, parts):
    vmem = pl.BlockSpec(memory_space=pltpu.VMEM)
    rows, columns = parts[0].shape
    return pl.pallas_call(
        assemble_kernel,
        in_specs=[pl.BlockSpec(memory_space=pltpu.SMEM)] + [vmem] * len(parts),
        out_specs=vmem,
        out_shape=jax.ShapeDtypeStruct(((rows - BELOW) * len(parts), columns), bf16),
        compiler_params=pltpu.CompilerParams(vmem_limit_bytes=VMEM),
        cost_estimate=pl.CostEstimate(flops=1_000_000, bytes_accessed=1_000_000, transcendentals=0),
        name="assembled",
    )(place, *parts)


def split_kernel(ranks, core, tokens, mine, sent):
    batch, piece, width = tokens.shape
    half = batch // 2
    rows = width // ranks
    first = core[0] == 0
    for b in range(batch):
        parts = [
            jnp.concatenate(
                [
                    tokens[b, :, c * rows : (c + 1) * rows].astype(f32)
                    for c in range(k, ranks, 2)
                ],
                axis=1,
            )
            for k in range(2)
        ]
        own = jnp.where(first, parts[0], parts[1])
        other = jnp.where(first, parts[1], parts[0])
        here = first if b < half else jnp.logical_not(first)

        @pl.when(here)
        def _():
            mine[b % half] = jnp.concatenate([own, other], axis=1).astype(bf16)

        @pl.when(jnp.logical_not(here))
        def _():
            sent[b % half] = jnp.concatenate([other, own], axis=1).astype(bf16)


def split_tokens(core, tokens, ranks):
    batch, piece, width = tokens.shape
    vmem = pl.BlockSpec(memory_space=pltpu.VMEM)
    shape = jax.ShapeDtypeStruct((batch // 2, piece, width), bf16)
    return pl.pallas_call(
        lambda *refs: split_kernel(ranks, *refs),
        in_specs=[pl.BlockSpec(memory_space=pltpu.SMEM), vmem],
        out_specs=[vmem, vmem],
        out_shape=[shape, shape],
        compiler_params=pltpu.CompilerParams(vmem_limit_bytes=VMEM),
        cost_estimate=pl.CostEstimate(flops=1_000_000, bytes_accessed=1_000_000, transcendentals=0),
        name="split_tokens",
    )(core, tokens)


def distinct(pieces):
    arrays, where = [], []
    for array, index in pieces:
        found = [k for k, a in enumerate(arrays) if a is array]
        if not found:
            arrays.append(array)
            found = [len(arrays) - 1]
        where.append((found[0], index))
    return arrays, where


def rows_call(kernel, pieces, extra, name):
    arrays, where = distinct(pieces)
    vmem = pl.BlockSpec(memory_space=pltpu.VMEM)
    rows, width = arrays[0].shape[1:]
    return pl.pallas_call(
        lambda *refs: kernel(where, *refs),
        in_specs=[vmem] * (len(arrays) + len(extra)),
        out_specs=vmem,
        out_shape=jax.ShapeDtypeStruct((rows * len(where), width), bf16),
        compiler_params=pltpu.CompilerParams(vmem_limit_bytes=VMEM),
        cost_estimate=pl.CostEstimate(flops=1_000_000, bytes_accessed=1_000_000, transcendentals=0),
        name=name,
    )(*extra, *arrays)


def project_kernel(where, gain, columns, *refs):
    pieces, (out, projected) = refs[:-2], refs[-2:]
    rows = pieces[0].shape[1]

    @pl.when(pl.program_id(0) == 0)
    def _():
        for k, (a, index) in enumerate(where):
            values = pieces[a][index].astype(f32)
            scale = lax.rsqrt(jnp.mean(values * values, axis=1, keepdims=True) + EPSILON)
            out[k * rows : (k + 1) * rows, :] = (values * scale * gain[...]).astype(bf16)

    tile = 256
    for k in range(out.shape[0] // tile):
        at = slice(k * tile, (k + 1) * tile)
        projected[at, :] = dot(out[at, :], columns[...])


def project(pieces, gain, columns):
    arrays, where = distinct(pieces)
    rows, width = arrays[0].shape[1:]
    length, wide = rows * len(where), columns.shape[1]
    tile = 384 if wide % 384 == 0 else LANES

    def whole(shape):
        return pl.BlockSpec(shape, lambda i: (0,) * len(shape))

    return pl.pallas_call(
        lambda *refs: project_kernel(where, *refs),
        grid=(wide // tile,),
        in_specs=[whole(gain.shape), pl.BlockSpec((width, tile), lambda i: (0, i))]
        + [whole(a.shape) for a in arrays],
        out_specs=[whole((length, width)), pl.BlockSpec((length, tile), lambda i: (0, i))],
        out_shape=[
            jax.ShapeDtypeStruct((length, width), bf16),
            jax.ShapeDtypeStruct((length, wide), f32),
        ],
        compiler_params=pltpu.CompilerParams(vmem_limit_bytes=VMEM),
        cost_estimate=pl.CostEstimate(flops=1_000_000, bytes_accessed=1_000_000, transcendentals=0),
        name="project",
    )(gain, columns, *arrays)


def joined_kernel(where, *refs):
    pieces, out = refs[:-1], refs[-1]
    rows = pieces[0].shape[1]
    for k, (a, index) in enumerate(where):
        out[k * rows : (k + 1) * rows, :] = pieces[a][index]


def joined_rows(pieces):
    return rows_call(joined_kernel, pieces, [], "joined_rows")


def gate_kernel(result, projected, g_mixed, norms, by_channel, g_result, g_gate, mixed):
    local = result.shape[1]
    gain = by_channel[5:6, 0:local]
    r = norms[:, 0:1]
    y = result[...]
    gate = projected[...]
    gate_s = sigmoid(gate)
    silu = gate * gate_s
    gated = y * silu
    mixed[...] = (gated * r * gain).astype(bf16)
    g_gated = r * gain * g_mixed[...] - gated * norms[:, 1:2]
    g_result[...] = (g_gated * silu).astype(bf16)
    g_gate[...] = (g_gated * y * gate_s * (1.0 + gate * (1.0 - gate_s))).astype(bf16)


def gate_gradients(result, projected, g_mixed, norms, by_channel):
    length, local = result.shape
    width = 256

    def here(i):
        return (i, 0)

    block = pl.BlockSpec((width, local), here)
    return pl.pallas_call(
        gate_kernel,
        grid=(length // width,),
        in_specs=[
            block,
            block,
            block,
            pl.BlockSpec((width, 2), here),
            pl.BlockSpec(by_channel.shape, lambda i: (0, 0)),
        ],
        out_specs=[block] * 3,
        out_shape=[jax.ShapeDtypeStruct((length, local), bf16)] * 3,
        compiler_params=pltpu.CompilerParams(vmem_limit_bytes=VMEM),
        cost_estimate=pl.CostEstimate(flops=1_000_000, bytes_accessed=1_000_000, transcendentals=0),
        name="gate_gradients",
    )(result, projected, g_mixed, norms, by_channel)


def output_kernel(core, tokens, kept, got, output):
    batch = tokens.shape[0]
    half = batch // 2
    for b in range(batch):
        mine = core[0] == b // half
        total = jnp.where(mine, kept[b % half], got[b % half].astype(f32))
        output[b] = (tokens[b].astype(f32) + total).astype(bf16)


def token_kernel(ranks, core, tokens, cotangent, gain, kept, got, gradient):
    batch, _, width = tokens.shape
    half, side, rows = batch // 2, width // 2, width // ranks
    gains = (gain[:, :side], gain[:, side:])
    first = core[0] == 0
    gains = (jnp.where(first, gains[0], gains[1]), jnp.where(first, gains[1], gains[0]))
    for b in range(batch):
        owner = b // half
        g = jnp.where(core[0] == owner, kept[b % half], got[b % half].astype(f32))
        parts = (g[:, :side], g[:, side:]) if owner == 0 else (g[:, side:], g[:, :side])
        parts = (parts[0] * gains[0], parts[1] * gains[1])
        weighted = jnp.concatenate(
            [part[:, c * rows : (c + 1) * rows] for c in range(ranks // 2) for part in parts],
            axis=1,
        )
        values = tokens[b].astype(f32)
        scale = lax.rsqrt(jnp.mean(values * values, axis=1, keepdims=True) + EPSILON)
        inner = jnp.mean(values * weighted, axis=1, keepdims=True)
        gradient[b] = (
            cotangent[b].astype(f32) + scale * weighted - values * (scale * scale * scale * inner)
        )


def share_kernel(chips, place, summed, *parts):
    share, columns = parts[0].shape
    width = summed.shape[1]
    for j in range(chips):
        c = place[0] ^ j
        for k in range(columns // width):
            at = pl.multiple_of((k * chips + c) * share, share)
            parts[j][:, k * width : (k + 1) * width] = summed[pl.ds(at, share), :]


def shares_by_chip(place, summed, chips, share, columns):
    vmem = pl.BlockSpec(memory_space=pltpu.VMEM)
    return pl.pallas_call(
        lambda *refs: share_kernel(chips, *refs),
        in_specs=[pl.BlockSpec(memory_space=pltpu.SMEM), vmem],
        out_specs=[vmem] * chips,
        out_shape=[jax.ShapeDtypeStruct((share, columns), bf16)] * chips,
        compiler_params=pltpu.CompilerParams(vmem_limit_bytes=VMEM),
        cost_estimate=pl.CostEstimate(flops=1_000_000, bytes_accessed=1_000_000, transcendentals=0),
        name="shares_by_chip",
    )(place, summed)


def early_kernel(across, place, summed, *refs):
    parts, out = refs[:-1], refs[-1]
    share, local = parts[0].shape
    chips = len(parts)
    inner = chips * local
    for j, part in enumerate(parts):
        out[:, pl.ds(pl.multiple_of((place[0] ^ j) * local, LANES), local)] = part[...]
    rounds = (summed.shape[0] // share - chips) // across
    for k in range(across):
        for r in range(rounds):
            start = chips * share + (k * rounds + r) * share
            to = inner + (r * across + k) * local
            out[:, to : to + local] = summed[start : start + share, :]


def late_kernel(heads, place, *refs):
    parts, out = refs[:-1], refs[-1]
    chips = len(parts)
    each = heads // chips
    columns = parts[0].shape[1]
    local = columns - 2 * N - LANES
    inner = chips * local
    row = lax.broadcasted_iota(jnp.int32, (LANES, heads), 0)
    lane = lax.broadcasted_iota(jnp.int32, (LANES, heads), 1)
    steps = jnp.zeros((out.shape[0], heads), f32)
    shared = jnp.zeros((out.shape[0], 2 * N), f32)
    for j, part in enumerate(parts):
        c = place[0] ^ j
        out[:, pl.ds(pl.multiple_of(c * local, LANES), local)] = part[:, 0:local]
        shared = shared + part[:, local : local + 2 * N].astype(f32)
        pick = jnp.logical_and(lane == c * each + row, row < each)
        steps = steps + dot(part[:, local + 2 * N :], jnp.where(pick, 1.0, 0.0).astype(bf16))
    out[:, inner : inner + 2 * N] = shared.astype(bf16)
    out[:, inner + 2 * N :] = steps.astype(bf16)


def joined_shares(kernel, place, arrays, shape, name):
    vmem = pl.BlockSpec(memory_space=pltpu.VMEM)
    return pl.pallas_call(
        kernel,
        in_specs=[pl.BlockSpec(memory_space=pltpu.SMEM)] + [vmem] * len(arrays),
        out_specs=vmem,
        out_shape=jax.ShapeDtypeStruct(shape, bf16),
        compiler_params=pltpu.CompilerParams(vmem_limit_bytes=VMEM),
        cost_estimate=pl.CostEstimate(flops=1_000_000, bytes_accessed=1_000_000, transcendentals=0),
        name=name,
    )(place, *arrays)


def weights_kernel(early, rest, in_weight, step_weight, total_in, total_step, by_gain):
    inner = in_weight.shape[1] - 2 * N - early_columns(in_weight)
    heads = step_weight.shape[1]
    first = early[:, 0:inner].astype(f32)
    last = rest[:, 0 : inner + 2 * N].astype(f32)
    step = rest[:, inner + 2 * N :].astype(f32)
    total_in[:, 0:inner] = first
    total_in[:, inner:] = last
    total_step[...] = step
    by_gain[...] = (
        jnp.sum(in_weight[:, 0:inner].astype(f32) * first, axis=1, keepdims=True)
        + jnp.sum(in_weight[:, inner:].astype(f32) * last, axis=1, keepdims=True)
        + jnp.sum(step_weight[...].astype(f32) * step, axis=1, keepdims=True)
    )


def early_columns(in_weight):
    return (in_weight.shape[1] - 2 * N) // 2


def weight_totals(early, rest, in_weight, step_weight):
    rows = in_weight.shape[0]
    block = rows // 4 if rows % 64 == 0 else rows

    def here(i):
        return (i, 0)

    arrays = [early, rest, in_weight, step_weight]
    widths = [in_weight.shape[1], step_weight.shape[1], 1]
    return pl.pallas_call(
        weights_kernel,
        grid=(rows // block,),
        in_specs=[pl.BlockSpec((block, a.shape[1]), here) for a in arrays],
        out_specs=[pl.BlockSpec((block, width), here) for width in widths],
        out_shape=[jax.ShapeDtypeStruct((rows, width), f32) for width in widths],
        compiler_params=pltpu.CompilerParams(vmem_limit_bytes=VMEM),
        cost_estimate=pl.CostEstimate(flops=1_000_000, bytes_accessed=1_000_000, transcendentals=0),
        name="weight_totals",
    )(*arrays)


def whole_call(kernel, scalar, arrays, shape, dtype, name):
    vmem = pl.BlockSpec(memory_space=pltpu.VMEM)
    return pl.pallas_call(
        kernel,
        in_specs=[pl.BlockSpec(memory_space=pltpu.SMEM)] + [vmem] * len(arrays),
        out_specs=vmem,
        out_shape=jax.ShapeDtypeStruct(shape, dtype),
        compiler_params=pltpu.CompilerParams(vmem_limit_bytes=VMEM),
        cost_estimate=pl.CostEstimate(flops=1_000_000, bytes_accessed=1_000_000, transcendentals=0),
        name=name,
    )(scalar, *arrays)


def across_chips(x, bit):
    return lax.ppermute(x, "chip", [(i, i ^ bit) for i in range(lax.axis_size("chip"))])


def sibling(x):
    return lax.ppermute(x, "core", [(0, 1), (1, 0)])


def chip_bits(turn):
    chips = lax.axis_size("chip")
    bits = [1 << k for k in range(chips.bit_length() - 1)]
    return bits if turn == 0 else bits[::-1]


def after(x, *deps):
    return lax.optimization_barrier((x, deps))[0]


class Gather:
    def __init__(self, block):
        self.own = {bit: across_chips(block, bit) for bit in chip_bits(0)}
        self.have = []
        for turn in range(2):
            have = {0: (block, turn)}
            for bit in chip_bits(turn)[:1]:
                have[bit] = (self.own[bit], turn)
            self.have.append(have)

    def received(self):
        return list(self.own.values())

    def relay(self, *deps):
        relayed = []
        for turn, have in enumerate(self.have):
            for bit in chip_bits(turn)[1:]:
                new = {bit: (self.own[bit], turn)}
                for j, (array, index) in sorted(have.items()):
                    if j:
                        part = array[index : index + 1]
                        part = after(part, *deps) if deps else part
                        relayed.append(part)
                        new[j ^ bit] = (across_chips(part, bit), 0)
                have.update(new)
        return relayed

    def slots(self):
        return [self.have[turn][j] for turn, j in slot_order(len(self.have[0]))]


class Scatter:
    def __init__(self, rows, chips, *deps, keep_rows=None):
        self.rows = keep_rows or rows
        self.bits = [chip_bits(turn)[::-1] for turn in range(2)]
        gives = tuple(part.astype(bf16) for part in rows(True))
        self.gives = after(gives, *deps) if deps else gives
        self.kept = None
        self.sent = [across_chips(x, bits[0]) for x, bits in zip(self.gives, self.bits)]

    def step(self, *deps):
        kept = self.rows(False) if self.kept is None else self.kept
        sent = after(tuple(self.sent), *deps) if deps else self.sent
        self.kept, self.sent = [], []
        for turn, bits in enumerate(self.bits):
            bits.pop(0)
            total = kept[turn].astype(f32) + sent[turn].astype(f32)
            if bits:
                half = total.shape[0] // 2
                self.kept.append(total[:half])
                self.sent.append(across_chips(total[half:].astype(bf16), bits[0]))
            else:
                self.kept.append(total)

    def done(self, *deps):
        while self.bits[0]:
            self.step(*deps)
        return [part[0] for part in self.kept]


def chip_total(x):
    order = slot_order(x.shape[-2] // 2)
    for bit in chip_bits(0):
        moved = [order.index((turn, j ^ bit)) for turn, j in order]
        pick = jnp.asarray([[float(m == k) for k in range(len(order))] for m in moved], f32)
        x = x + jnp.einsum("st,atp->asp", pick, across_chips(x, bit), precision=precise)
    return x


def across_groups(x, step):
    return lax.ppermute(x, "dp", [(i, i ^ step) for i in range(lax.axis_size("dp"))])


def by_group(x):
    blocks, rows, width = x.shape
    count = lax.axis_size("dp")
    return x.reshape(blocks, count, rows // count, width).transpose(1, 0, 2, 3)


def group_scatter(x):
    return lax.psum_scatter(x, "dp", scatter_dimension=0, tiled=False)


def group_gather(x):
    return lax.all_gather(x, "dp", axis=0, tiled=True)


def body(
    tokens,
    norm_gain,
    in_weight,
    step_weight,
    filter_weight,
    filter_bias,
    step_bias,
    log_rate,
    skip_scale,
    inner_gain,
    out_weight,
    cotangent,
):
    chips = lax.axis_size("chip")
    chip, core = lax.axis_index("chip"), lax.axis_index("core")
    rank = chip * 2 + core
    batch, piece, width = tokens.shape
    half = batch // 2
    ranks = chips * 2
    heads = log_rate.shape[0] * ranks
    inner = inner_gain.shape[0] * ranks
    local_heads, local = heads // chips, inner // chips
    rows = in_weight.shape[0]
    side = width // 2
    taps = filter_weight.shape[0]
    channels = local + 2 * N
    first = core == 0

    def own_first(a, b):
        return (jnp.where(first, a, b), jnp.where(first, b, a))

    columns_in = 2 * local + 2 * N + LANES
    place = jnp.stack([chip, core]).astype(jnp.int32)
    per_head = jnp.stack([step_bias, log_rate, skip_scale])
    per_head = jnp.pad(per_head, ((0, 5), (0, 0)))
    packed_weight = pack_columns(
        place,
        [
            in_weight,
            step_weight,
            filter_weight,
            filter_bias[None],
            inner_gain[None],
            norm_gain[None],
        ],
        per_head,
        chips,
        columns_in,
        inner,
    )

    def of_core(a, which):
        return lax.dynamic_slice_in_dim(a, which * half, half, 0)

    core_ref = core.astype(jnp.int32).reshape(1)
    mine, sent = split_tokens(after(core_ref, *packed_weight), tokens, ranks)
    got = sibling(sent)
    token_blocks = [jnp.stack([mine[b], got[b]]) for b in range(half)]
    mine_cot, got_cot = of_core(cotangent, core), sibling(of_core(cotangent, 1 - core))
    cot_blocks = [jnp.stack([mine_cot[b], got_cot[b]]) for b in range(half)]

    parts = [across_chips(part, j) if j else part for j, part in enumerate(packed_weight)]
    parts = parts + [sibling(part) for part in parts]
    by_channel, by_head, gain = parameters(parts, channels, width)
    columns = assembled(place, parts)
    out_low, out_high = own_first(out_weight, sibling(out_weight))
    out_rows = jnp.concatenate([out_low, out_high], axis=0)

    def tn(a, b):
        return lax.dot_general(a, b, (((0,), (0,)), ((), ())), preferred_element_type=f32)

    rank_ref = rank.astype(jnp.int32).reshape(1)
    spans = range(half)
    queue = [Gather(token_blocks[0])]
    for block in token_blocks[1:] + cot_blocks:
        queue.append((block, None))
    moved = 0

    def advance(*deps):
        nonlocal moved
        if moved >= len(queue):
            return []
        now = queue[moved]
        before = [part for part, _ in queue[moved - 1].slots()] if moved else []
        relayed = now.relay(*deps, *before)
        moved += 1
        if moved < len(queue):
            waits = now.received() if moved > 1 else [part for part, _ in now.slots()]
            block = after(queue[moved][0], *waits, *deps)
            queue[moved] = Gather(block)
            relayed = relayed + [block]
        return relayed

    def slot_rows(a, run):
        count = a.shape[0] // 2

        def rows(upper):
            part = run(a[:count] if upper else a[count:])
            return part.reshape(2, chips // 2, piece, width)

        return rows

    advance()
    normed, projected, fronts = [], [], []
    for b in spans:
        ready = after(gain, fronts[b - 1][2]) if b else gain
        normed_b, projected_b = project(queue[b].slots(), ready, columns)
        normed.append(normed_b)
        projected.append(projected_b)
        issued = advance(*([projected[0]] if b == 0 else []))
        fronts.append(
            scan_forward(
                rank_ref, projected[b], by_channel, after(by_head, *issued), local, piece
            )
        )
        if b + 1 < half:
            advance(fronts[b][2])
    while moved < len(queue):
        advance(fronts[-1][2])
    cots = queue[half:]

    all_cot, g_mixed, stats = [], [], []
    for b in spans:
        result, scaled, squares, states = fronts[b]
        all_cot.append(joined_rows(cots[b].slots()))
        g_mixed.append(dot_nt(all_cot[b], out_rows))
        both = jnp.stack([squares[:, 0], jnp.sum(scaled.astype(f32) * g_mixed[b], axis=1)])
        stats.append(chip_total(both.reshape(2, ranks, piece)).reshape(both.shape) / inner)
    g_results, g_gates, mixed, outs = [], [], [], []
    for b in spans:
        r = lax.rsqrt(stats[b][0] + EPSILON)
        norms = jnp.stack([r, r * r * r * stats[b][1]], axis=1)
        if b + 1 < half:
            norms = after(norms, *cots[b + 1].received())
        g_result, g_gate, mixed_b = gate_gradients(
            fronts[b][0], projected[b], g_mixed[b], norms, by_channel
        )
        g_results.append(g_result)
        g_gates.append(g_gate)
        mixed.append(mixed_b)
        outs.append(Scatter(slot_rows(mixed_b, lambda x: dot(x, out_rows)), chips))

    def row_sums(parts):
        far = [tn(normed[b][:, side:], parts[b]) for b in range(len(parts))]
        near = [tn(normed[b][:, :side], parts[b]) for b in range(len(parts))]
        return far, near

    def core_sum(far, near, *deps):
        sent = after(sum(far).astype(bf16), *deps)
        total = (sum(near) + sibling(sent).astype(f32)).astype(bf16)
        return total.reshape(chips, rows, -1)

    def by_chip(near):
        found = []
        for j in range(chips):
            part = lax.dynamic_index_in_dim(near, chip ^ j, 0, keepdims=True)
            found.append(across_chips(part, j) if j else part)
        return found

    def exchanged(parts):
        return [across_chips(part, j) if j else part for j, part in enumerate(parts)]

    def in_place(parts, size, total):
        whole = jnp.zeros(parts[0].shape[:2] + (total,), bf16)
        for j, part in enumerate(parts):
            whole = lax.dynamic_update_slice_in_dim(whole, part[:, :, :size], (chip ^ j) * size, 2)
        return whole

    gate_near = core_sum(*row_sums(g_gates))
    out_gradient = sum(tn(mixed[b], all_cot[b]) for b in spans)
    out_near, out_far = own_first(out_gradient[: local // 2], out_gradient[local // 2 :])
    out_near = (out_near + sibling(out_far.astype(bf16)).astype(f32)).astype(bf16)
    groups = lax.axis_size("dp")
    share = rows // groups
    out_near = out_near.reshape(groups, -1, width)
    out_near = jnp.concatenate(
        [out_near[:, :, k : k + local] for k in range(0, width, local)], axis=1
    )
    gate_near = by_group(gate_near).reshape(groups, -1, local)
    early = group_scatter(jnp.concatenate([gate_near, out_near], axis=1))

    g_columns, sums, g_normed, far, near = [], [], [], [], []
    ready = after(by_head, gate_near, out_near, *[x for out in outs for x in out.gives])
    for b in spans:
        g_proj, sum_channel, sum_head = scan_backward(
            rank_ref, projected[b], g_results[b], g_gates[b], fronts[b][3], by_channel, ready, piece
        )
        if b == half - 1:
            g_proj, sum_channel, sum_head = after((g_proj, sum_channel, sum_head), early)
        g_columns.append(g_proj)
        sums.append((sum_channel, sum_head))
        waits = [sum_head]
        for part in outs if b == 0 else g_normed[:b]:
            part.step(sum_head)
        rest = g_proj[:, local:]
        far.append(tn(normed[b][:, side:], rest))
        near.append(tn(normed[b][:, :side], rest))
        if b == 0:
            early = after(early, sum_head)
        if b == half - 1:
            rest_near = core_sum(far, near)
        send = slot_rows(g_proj, lambda x: dot_nt(x, columns))
        late = after(g_proj, rest_near) if b == half - 1 else g_proj
        keep = slot_rows(late, lambda x: dot_nt(x, columns))
        g_normed.append(Scatter(send, chips, *([early] if b == 0 else []), keep_rows=keep))
        if b == 0:
            if share % 16 == 0:
                gate_parts = exchanged(shares_by_chip(place, early, chips, share, local))
                early = joined_shares(
                    lambda *refs: early_kernel(width // local, *refs),
                    place,
                    [early, *gate_parts],
                    (share, 2 * inner),
                    "early_share",
                )
            else:
                gate_parts = by_chip(early[: chips * share].reshape(chips, share, local))
                out_share = jnp.split(early[chips * share :], width // local)
                out_share = jnp.concatenate(out_share, axis=1)
                early = [in_place(gate_parts, local, inner)[0]]
                early = early + jnp.split(out_share, inner // width)
                early = jnp.concatenate(early, axis=1)
            out_sums = [out.done() for out in outs]
            waits = [early] + [x for part in out_sums for x in part]
            early = group_gather(early)
        ready = after(by_head, far[b], near[b], *g_normed[b].gives, *waits)
    early = after(early, rest_near)
    total_out = early[:, inner:].reshape(groups, share, -1, width)
    total_out = total_out.transpose(0, 2, 1, 3).reshape(-1, width)
    late_columns = 2 * N + LANES
    rest_blocks = by_group(rest_near).reshape(groups, -1, local + late_columns)
    if local % late_columns == 0:
        cuts = range(0, local + late_columns, late_columns)
        rest_blocks = [rest_blocks[:, :, k : k + late_columns] for k in cuts]
        rest_sum = group_scatter(jnp.concatenate(rest_blocks, axis=1))
    else:
        cuts = [0]
        rest_sum = group_scatter(rest_blocks)
    if share % 16 == 0:
        rest_parts = shares_by_chip(place, rest_sum, chips, share, local + late_columns)
        rest_total = joined_shares(
            lambda *refs: late_kernel(heads, *refs),
            place,
            exchanged(rest_parts),
            (share, inner + 2 * N + heads),
            "late_share",
        )
    else:
        rest_sum = jnp.concatenate(jnp.split(rest_sum, len(cuts)), axis=1)
        rest_parts = by_chip(rest_sum.reshape(chips, share, -1))
        shared = sum(part[:, :, local : local + 2 * N].astype(f32) for part in rest_parts)
        step_parts = [part[:, :, local + 2 * N :] for part in rest_parts]
        rest_total = jnp.concatenate(
            [
                in_place(rest_parts, local, inner),
                shared.astype(bf16),
                in_place(step_parts, local_heads, heads),
            ],
            axis=2,
        )[0]
    rest_total = group_gather(rest_total)
    total_out = total_out.astype(f32)

    total_in, total_step, total_gain = weight_totals(early, rest_total, in_weight, step_weight)
    total_gain = total_gain[:, 0] / norm_gain.astype(f32)
    total_inner = jnp.sum(out_weight.astype(f32) * total_out, axis=1) / inner_gain.astype(f32)

    def regrouped(parts):
        kept = jnp.stack([part[0] for part in parts])
        got = sibling(jnp.stack([part[1] for part in parts]).astype(bf16))
        return (kept, got)

    g_normed = [part.done(rest_near) for part in g_normed]

    sum_channel = sum(part[0] for part in sums)
    sum_head = sum(part[1] for part in sums)

    def placed(a, size):
        empty = jnp.zeros((a.shape[0], size), f32)
        return lax.dynamic_update_slice_in_dim(empty, a, chip * a.shape[1], 1)

    skip = jnp.sum(sum_channel[5, :local].reshape(local_heads, HEAD), axis=1)[None]
    packed = jnp.concatenate(
        [
            jnp.concatenate(
                [placed(sum_channel[: taps + 1, :local], inner), sum_channel[: taps + 1, local:]],
                axis=1,
            ).reshape(-1),
            placed(jnp.concatenate([sum_head[:2, :local_heads], skip], axis=0), heads).reshape(-1),
        ]
    )
    packed = jnp.pad(packed, (0, -packed.shape[0] % 1024)).reshape(-1, LANES)
    packed = after(packed, rest_near)
    packed = packed + sibling(packed)
    for bit in chip_bits(0):
        packed = packed + across_chips(packed, bit)
    for bit in [1 << k for k in range(lax.axis_size("dp").bit_length() - 1)]:
        packed = packed + across_groups(packed, bit)
    packed = packed.reshape(-1)
    cut = (taps + 1) * (inner + 2 * N)

    def own_of(a):
        size = a.shape[1] // ranks
        return lax.dynamic_slice_in_dim(a, rank * size, size, 1)

    channel_totals = own_of(packed[:cut].reshape(taps + 1, -1))
    head_totals = own_of(packed[cut : cut + 3 * heads].reshape(3, heads))

    kept, got = regrouped(out_sums)
    output = whole_call(output_kernel, core_ref, [tokens, kept, got], tokens.shape, bf16, "output")
    kept, got = regrouped(g_normed)
    token_gradient = whole_call(
        lambda *refs: token_kernel(ranks, *refs),
        core_ref,
        [tokens, cotangent, gain, kept, got],
        tokens.shape,
        f32,
        "token_gradient",
    )
    return (
        output,
        token_gradient,
        total_gain,
        total_in,
        total_step,
        channel_totals[:taps],
        channel_totals[taps],
        head_totals[0],
        head_totals[1],
        head_totals[2],
        total_inner,
        total_out,
    )


def solution(mesh):
    ranks, groups = mesh.shape["sp"], mesh.shape["dp"]
    fine = Mesh(mesh.devices.reshape(ranks // 2, 2, groups), ("chip", "core", "dp"))
    sp = ("chip", "core")
    return jax.shard_map(
        body,
        mesh=fine,
        in_specs=(
            P("dp", sp, None),
            P(sp),
            P(sp, None),
            P(sp, None),
            P(None, sp),
            P(sp),
            P(sp),
            P(sp),
            P(sp),
            P(sp),
            P(sp, None),
            P("dp", sp, None),
        ),
        out_specs=(
            P("dp", sp, None),
            P("dp", sp, None),
            P(sp),
            P(sp, None),
            P(sp, None),
            P(None, sp),
            P(sp),
            P(sp),
            P(sp),
            P(sp),
            P(sp),
            P(sp, None),
        ),
        check_vma=False,
    )
```

```python
import jax
import jax.numpy as jnp
from jax import lax
from jax.experimental import pallas as pl
from jax.experimental.pallas import tpu as pltpu
from jax.sharding import Mesh, PartitionSpec as P

N = 128
HEAD = 64
LANES = 128
VMEM = 60 * 1024 * 1024
EPSILON = 1e-05
f32, bf16 = jnp.float32, jnp.bfloat16
precise = lax.Precision.HIGHEST


def sigmoid(v):
    return 0.5 * jnp.tanh(0.5 * v) + 0.5


def dot(a, b):
    return jnp.dot(a, b, preferred_element_type=f32)


def dot_nt(a, b):
    return lax.dot_general(a, b, (((1,), (1,)), ((), ())), preferred_element_type=f32)


def spread_pair(low, a, p):
    return jnp.where(low, a[:, 2 * p : 2 * p + 1], a[:, 2 * p + 1 : 2 * p + 2])


def stacked(low, a):
    zero = jnp.zeros_like(a)
    return jnp.concatenate([jnp.where(low, a, zero), jnp.where(low, zero, a)], axis=0).astype(bf16)


def running_sum(x):
    rows = lax.broadcasted_iota(jnp.int32, x.shape, 0)
    k = 1
    while k < x.shape[0]:
        x = x + jnp.where(rows >= k, pltpu.roll(x, k, 0), 0.0)
        k *= 2
    return x


def forward_kernel(
    rank, projected, by_channel, by_head, result, scaled, squares, states, state, window
):
    step = pl.program_id(0)
    width, local = result.shape
    channels = local + 2 * N
    taps = 4

    @pl.when(step == 0)
    def _():
        state[...] = jnp.zeros_like(state)
        window[0:8, :] = jnp.zeros((8, channels), f32)

    @pl.when(step > 0)
    def _():
        window[0:8, :] = window[width : width + 8, :]

    window[8 : 8 + width, :] = projected[:, local : local + channels]
    filtered = by_channel[4:5, :]
    for tap in range(taps):
        at = 9 - taps + tap
        filtered = filtered + by_channel[tap : tap + 1, :] * window[at : at + width, :]
    active = filtered * sigmoid(filtered)
    entry = active[:, local : local + N]
    readout = active[:, local + N :].astype(bf16)
    steps = jax.nn.softplus(projected[:, local + channels :] + by_head[0:1, :])
    rows = lax.broadcasted_iota(jnp.int32, (width, width), 0)
    cols = lax.broadcasted_iota(jnp.int32, (width, width), 1)
    running = running_sum(steps * by_head[1:2, :])
    across = running.T
    meeting = jnp.where(cols <= rows, dot_nt(readout, entry.astype(bf16)), 0.0)
    before = state[...].astype(bf16)
    states[0] = before
    carried = dot(readout, before)
    entry_t = entry.T.astype(bf16)
    low = lax.broadcasted_iota(jnp.int32, (width, LANES), 1) < HEAD
    total = jnp.zeros((width, LANES), f32)
    weighted, decay = [], []
    for p in range(local // LANES):
        at = slice(p * LANES, (p + 1) * LANES)
        signal = active[:, at]
        mixing, along = [], []
        for h in (2 * p, 2 * p + 1):
            along.append(jnp.broadcast_to(running[:, h : h + 1], (width, width)))
            span = jnp.minimum(along[-1] - across[h : h + 1, :], 0.0)
            mixing.append((jnp.exp(span) * meeting).astype(bf16))
        entered = signal * spread_pair(low, steps, p)
        y = dot(jnp.concatenate(mixing, axis=1), stacked(low, entered))
        along = jnp.where(low, along[0], along[1])
        grown_p = jnp.exp(along)
        y = y + grown_p * carried[:, at] + by_channel[6:7, at] * signal
        result[:, at] = y
        gate = projected[:, at]
        gated = y * gate * sigmoid(gate)
        scaled[:, at] = (gated * by_channel[5:6, at]).astype(bf16)
        total = total + gated * gated
        weighted.append((entered * jnp.exp(along[width - 1 : width, :] - along)).astype(bf16))
        decay.append(grown_p[width - 1 : width, :])
    squares[...] = jnp.sum(total, axis=1, keepdims=True)
    state[...] = jnp.concatenate(decay, axis=1) * state[...] + dot(
        entry_t, jnp.concatenate(weighted, axis=1)
    )


def backward_kernel(
    rank,
    projected,
    tail,
    g_result,
    g_gate,
    states,
    by_channel,
    by_head,
    g_projected,
    sum_channel,
    sum_head,
    adjoint,
    window,
    ahead,
):
    step = pl.program_id(0)
    last = pl.num_programs(0) - 1
    width, local = g_result.shape
    channels = local + 2 * N
    taps = 4

    @pl.when(step == 0)
    def _():
        adjoint[...] = jnp.zeros_like(adjoint)
        ahead[width : width + 8, :] = jnp.zeros((8, channels), f32)
        sum_channel[...] = jnp.zeros_like(sum_channel)
        sum_head[...] = jnp.zeros_like(sum_head)

    @pl.when(step > 0)
    def _():
        ahead[width : width + 8, :] = ahead[0:8, :]

    window[0:8, :] = jnp.where(step == last, 0.0, tail[:, local : local + channels])
    window[8 : 8 + width, :] = projected[:, local : local + channels]
    filtered = by_channel[4:5, :]
    for tap in range(taps):
        at = 9 - taps + tap
        filtered = filtered + by_channel[tap : tap + 1, :] * window[at : at + width, :]
    gate_f = sigmoid(filtered)
    active = filtered * gate_f
    slope = gate_f * (1.0 + filtered * (1.0 - gate_f))
    entry = active[:, local : local + N]
    readout = active[:, local + N :]
    entry_b, readout_b = entry.astype(bf16), readout.astype(bf16)
    shifted = projected[:, local + channels :] + by_head[0:1, :]
    steps = jax.nn.softplus(shifted)
    rate = by_head[1:2, :]
    rows = lax.broadcasted_iota(jnp.int32, (width, width), 0)
    cols = lax.broadcasted_iota(jnp.int32, (width, width), 1)
    falls = steps * rate
    running = running_sum(falls)
    across = running.T
    meeting = jnp.where(rows <= cols, dot_nt(entry_b, readout_b), 0.0)
    before = states[0]
    after = adjoint[...].astype(bf16)
    carried = dot(readout_b, before)
    returned = dot(entry_b, after)
    readout_t = readout.T.astype(bf16)
    lane = lax.broadcasted_iota(jnp.int32, (width, LANES), 1)
    low = lane < HEAD
    g_projected[:, 0:local] = g_gate[...]
    ones = jnp.ones((width, LANES), bf16)
    by_col = jnp.zeros((width, LANES), f32)
    pick_rows = lax.broadcasted_iota(jnp.int32, (LANES, LANES), 0) // HEAD
    pick_cols = lax.broadcasted_iota(jnp.int32, (LANES, LANES), 1)
    g_meeting = jnp.zeros((width, width), f32)
    by_row = []
    per_head = jnp.zeros((3 * width + 8, LANES), f32)
    g_entry = jnp.zeros((width, N), f32)
    g_readout = jnp.zeros((width, N), f32)
    for p in range(local // LANES):
        at = slice(p * LANES, (p + 1) * LANES)
        signal = active[:, at]
        g_y = g_result[:, at].astype(f32)
        steps_p = spread_pair(low, steps, p)
        entered = signal * steps_p
        g_mixing = dot_nt(stacked(low, entered), g_result[:, at])
        mixing, along, parts = [], [], []
        for k, h in enumerate((2 * p, 2 * p + 1)):
            along.append(jnp.broadcast_to(running[:, h : h + 1], (width, width)))
            span = jnp.minimum(across[h : h + 1, :] - along[-1], 0.0)
            kernel = jnp.exp(span)
            mixing.append((kernel * meeting).astype(bf16))
            part = g_mixing[k * width : (k + 1) * width, :] * kernel
            g_meeting = g_meeting + part
            parts.append((part * meeting).astype(bf16))
            by_row.append(jnp.sum(parts[-1].astype(f32), axis=0, keepdims=True))
        across_sum = dot(jnp.concatenate(parts, axis=0), ones)
        for k, h in enumerate((2 * p, 2 * p + 1)):
            by_col = jnp.where(lane == h, across_sum[k * width : (k + 1) * width], by_col)
        along = jnp.where(low, along[0], along[1])
        grown_p = jnp.exp(along)
        left_p = jnp.exp(along[width - 1 : width, :] - along)
        back = left_p * returned[:, at]
        through = dot(jnp.concatenate(mixing, axis=1), stacked(low, g_y)) + back
        skip = by_channel[6:7, at]
        ahead[0:width, at] = steps_p * through + skip * g_y
        sum_channel[5:6, at] += jnp.sum(g_y * signal, axis=0, keepdims=True)
        g_grown = grown_p * g_y
        g_grown_b = g_grown.astype(bf16)
        before_p = before[:, at]
        after_p = adjoint[:, at]
        held = jnp.sum(after_p * before_p.astype(f32), axis=0, keepdims=True)
        pieces = jnp.concatenate(
            [
                signal * through,
                entered * back,
                g_grown * carried[:, at],
                jnp.broadcast_to(held, (8, LANES)),
            ],
            axis=0,
        )
        pick = jnp.where(pick_rows + 2 * p == pick_cols, 1.0, 0.0)
        per_head = per_head + dot(pieces.astype(bf16), pick.astype(bf16))
        g_readout = g_readout + dot_nt(g_grown_b, before_p)
        g_entry = g_entry + dot_nt((left_p * entered).astype(bf16), after[:, at])
        adjoint[:, at] = grown_p[width - 1 : width, :] * after_p + dot(readout_t, g_grown_b)
    g_meeting = jnp.where(rows <= cols, g_meeting, 0.0)
    g_readout = g_readout + dot(g_meeting.T.astype(bf16), entry_b)
    g_entry = g_entry + dot(g_meeting.astype(bf16), readout_b)
    heads = len(by_row)
    by_row = jnp.concatenate(by_row + [jnp.zeros((LANES - heads, width), f32)], axis=0).T
    direct = per_head[0:width]
    entering = per_head[width : 2 * width]
    rising = by_row + per_head[2 * width : 3 * width] - by_col
    change = entering - rising
    g_falls = (
        running_sum(change)
        - change
        + jnp.sum(rising, axis=0, keepdims=True)
        + jnp.exp(running[width - 1 : width, :]) * per_head[3 * width : 3 * width + 1]
    )
    g_steps = rate * g_falls + direct
    g_raw = g_steps * sigmoid(shifted)
    sum_head[0:1, :] += jnp.sum(g_raw, axis=0, keepdims=True)
    sum_head[1:2, :] += jnp.sum(falls * g_falls, axis=0, keepdims=True)
    g_projected[:, local + channels :] = g_raw.astype(bf16)
    ahead[0:width, local : local + N] = g_entry
    ahead[0:width, local + N :] = g_readout
    g_filtered = ahead[0:width, :] * slope
    ahead[0:width, :] = g_filtered
    g_in = jnp.zeros((width, channels), f32)
    for tap in range(taps):
        back_at = taps - 1 - tap
        g_in = g_in + by_channel[tap : tap + 1, :] * ahead[back_at : back_at + width, :]
        at = 9 - taps + tap
        sum_channel[tap : tap + 1, :] += jnp.sum(
            g_filtered * window[at : at + width, :], axis=0, keepdims=True
        )
    sum_channel[4:5, :] += jnp.sum(g_filtered, axis=0, keepdims=True)
    g_projected[:, local : local + channels] = g_in.astype(bf16)


def reversed_bits(chip, count):
    bits = count.bit_length() - 1
    return sum(((chip >> k) & 1) << (bits - 1 - k) for k in range(bits))


def slot_of(place, rank, pieces):
    count = pieces // 2
    half = count // 2
    core = (place ^ rank) & 1
    chip = (place ^ rank) >> 1
    at = jnp.where(core == 0, chip, reversed_bits(chip, count))
    return jnp.where(at < half, count, -half) + core * half + at


def chip_order(turn, count):
    return [j if turn == 0 else reversed_bits(j, count) for j in range(count)]


def slot_order(count):
    half = count // 2
    orders = [chip_order(turn, count) for turn in range(2)]
    return [
        (turn, orders[turn][upper * half + low])
        for upper in (1, 0)
        for turn in range(2)
        for low in range(half)
    ]


def scan_forward(rank, projected, by_channel, by_head, local, width):
    length, columns = projected.shape
    count = length // width
    channels = local + 2 * N

    def here(i, rank):
        return (slot_of(i, rank[0], count), 0)

    def fixed(i, rank):
        return (0, 0)

    return pl.pallas_call(
        forward_kernel,
        grid_spec=pltpu.PrefetchScalarGridSpec(
            num_scalar_prefetch=1,
            grid=(count,),
            in_specs=[
                pl.BlockSpec((width, columns), here),
                pl.BlockSpec((8, channels), fixed),
                pl.BlockSpec((8, LANES), fixed),
            ],
            out_specs=[
                pl.BlockSpec((width, local), here),
                pl.BlockSpec((width, local), here),
                pl.BlockSpec((width, 1), here),
                pl.BlockSpec((1, N, local), lambda i, rank: (i, 0, 0)),
            ],
            scratch_shapes=[
                pltpu.VMEM((N, local), f32),
                pltpu.VMEM((width + 8, channels), f32),
            ],
        ),
        out_shape=[
            jax.ShapeDtypeStruct((length, local), f32),
            jax.ShapeDtypeStruct((length, local), bf16),
            jax.ShapeDtypeStruct((length, 1), f32),
            jax.ShapeDtypeStruct((count, N, local), bf16),
        ],
        compiler_params=pltpu.CompilerParams(vmem_limit_bytes=VMEM),
        cost_estimate=pl.CostEstimate(flops=1_000_000, bytes_accessed=1_000_000, transcendentals=0),
        name="scan_forward",
    )(rank, projected, by_channel, by_head)


def scan_backward(rank, projected, g_result, g_gate, states, by_channel, by_head, width):
    length, columns = projected.shape
    local = g_result.shape[1]
    count = length // width
    channels = local + 2 * N

    def here(i, rank):
        return (slot_of(count - 1 - i, rank[0], count), 0)

    def tail(i, rank):
        earlier = jnp.maximum(count - 2 - i, 0)
        return (slot_of(earlier, rank[0], count) * (width // 8) + (width // 8 - 1), 0)

    def fixed(i, rank):
        return (0, 0)

    return pl.pallas_call(
        backward_kernel,
        grid_spec=pltpu.PrefetchScalarGridSpec(
            num_scalar_prefetch=1,
            grid=(count,),
            in_specs=[
                pl.BlockSpec((width, columns), here),
                pl.BlockSpec((8, columns), tail),
                pl.BlockSpec((width, local), here),
                pl.BlockSpec((width, local), here),
                pl.BlockSpec((1, N, local), lambda i, rank: (count - 1 - i, 0, 0)),
                pl.BlockSpec((8, channels), fixed),
                pl.BlockSpec((8, LANES), fixed),
            ],
            out_specs=[
                pl.BlockSpec((width, columns), here),
                pl.BlockSpec((8, channels), fixed),
                pl.BlockSpec((8, LANES), fixed),
            ],
            scratch_shapes=[
                pltpu.VMEM((N, local), f32),
                pltpu.VMEM((width + 8, channels), f32),
                pltpu.VMEM((width + 8, channels), f32),
            ],
        ),
        out_shape=[
            jax.ShapeDtypeStruct((length, columns), bf16),
            jax.ShapeDtypeStruct((8, channels), f32),
            jax.ShapeDtypeStruct((8, LANES), f32),
        ],
        compiler_params=pltpu.CompilerParams(vmem_limit_bytes=VMEM),
        cost_estimate=pl.CostEstimate(flops=1_000_000, bytes_accessed=1_000_000, transcendentals=0),
        name="scan_backward",
    )(rank, projected, projected, g_result, g_gate, states, by_channel, by_head)


BELOW = 16


def pack_kernel(
    place,
    in_weight,
    step_weight,
    filter_weight,
    filter_bias,
    inner_gain,
    norm_gain,
    per_head,
    *refs,
):
    parts, spread = refs[:-1], refs[-1]
    chips = len(parts)
    rows, columns = in_weight.shape[0], parts[0].shape[1]
    heads = step_weight.shape[1]
    local = (columns - 2 * N - LANES) // 2
    inner = local * chips
    channels = local + 2 * N
    each = heads // chips
    chip, core = place[0], place[1]
    taps, mine = filter_weight.shape
    at_row = lax.broadcasted_iota(jnp.int32, (heads, LANES), 0)
    at_lane = lax.broadcasted_iota(jnp.int32, (heads, LANES), 1)

    def laid(a, width, at):
        a = jnp.pad(a.astype(f32), ((0, 0), (0, width - a.shape[1])))
        return pltpu.roll(a, at, 1)

    filters = jnp.concatenate(
        [
            filter_weight[...].astype(f32),
            filter_bias[...].astype(f32),
            jnp.zeros((8 - taps - 1, mine), f32),
        ],
        axis=0,
    )
    spread[...] = laid(filters, spread.shape[1], (2 * chip + core) * mine)
    gain = laid(norm_gain[...], -(-chips * rows // LANES) * LANES, chip * rows)
    inner_row = laid(inner_gain[...], local, core * inner_gain.shape[1])
    head_rows = laid(per_head[...], LANES, core * (each // 2))
    for j in range(chips):
        c = chip ^ j
        out = parts[j]
        at = pl.ds(0, rows)
        from_gate = pl.ds(pl.multiple_of(c * local, LANES), local)
        out[at, 0:local] = in_weight[:, from_gate]
        out[at, local : 2 * local] = in_weight[
            :, pl.ds(pl.multiple_of(inner + c * local, LANES), local)
        ]
        out[at, 2 * local : 2 * local + 2 * N] = in_weight[:, 2 * inner :]
        pick = jnp.logical_and(at_row == c * each + at_lane, at_lane < each)
        pick = jnp.where(pick, 1.0, 0.0).astype(bf16)
        out[at, 2 * local + 2 * N :] = dot(step_weight[...], pick).astype(bf16)
        top = jnp.concatenate([spread[:, from_gate], spread[:, inner:]], axis=1)
        if j == 0:
            row = lax.broadcasted_iota(jnp.int32, (8, channels), 0)
            wide = jnp.pad(inner_row, ((0, 0), (0, 2 * N)))
            top = jnp.where(row == 5, wide, top)
        low = [jnp.zeros((8, LANES), f32) if j else head_rows, jnp.broadcast_to(gain, (8, gain.shape[1]))]
        low = jnp.concatenate(low, axis=1)
        low = jnp.pad(low, ((0, 0), (0, columns - low.shape[1])))
        top = jnp.pad(top, ((0, 0), (0, columns - channels)))
        out[rows:, :] = jnp.concatenate([top, low], axis=0).astype(bf16)


def pack_columns(place, arrays, per_head, chips, columns, inner):
    rows = arrays[0].shape[0] + BELOW
    vmem = pl.BlockSpec(memory_space=pltpu.VMEM)
    return pl.pallas_call(
        pack_kernel,
        in_specs=[pl.BlockSpec(memory_space=pltpu.SMEM)] + [vmem] * (len(arrays) + 1),
        out_specs=[vmem] * chips,
        out_shape=[jax.ShapeDtypeStruct((rows, columns), bf16)] * chips,
        scratch_shapes=[pltpu.VMEM((8, inner + 2 * N), f32)],
        compiler_params=pltpu.CompilerParams(vmem_limit_bytes=VMEM),
        cost_estimate=pl.CostEstimate(flops=1_000_000, bytes_accessed=1_000_000, transcendentals=0),
        name="pack_columns",
    )(place, *arrays, per_head)


def parameter_kernel(side, *refs):
    parts, (by_channel, by_head, gain) = refs[:-3], refs[-3:]
    channels = by_channel.shape[1]
    half = len(parts) // 2
    sums = [
        sum((part[...].astype(f32) for part in parts[k * half + 1 : (k + 1) * half]), parts[k * half][...].astype(f32))
        for k in range(2)
    ]
    whole = sums[0] + sums[1]
    heads = whole[8:16, 0:LANES]
    head = lax.broadcasted_iota(jnp.int32, (LANES, channels), 0)
    lane = lax.broadcasted_iota(jnp.int32, (LANES, channels), 1)
    expand = jnp.where(head == lane // HEAD, 1.0, 0.0).astype(bf16)
    skip = dot(heads[2:3].astype(bf16), expand)
    row = lax.broadcasted_iota(jnp.int32, (8, channels), 0)
    by_channel[...] = jnp.where(row == 6, skip, whole[0:8, 0:channels])
    row = lax.broadcasted_iota(jnp.int32, (8, LANES), 0)
    by_head[...] = jnp.where(
        row == 0, heads, jnp.where(row == 1, -jnp.exp(heads), 0.0)
    )
    gain[:, 0:side] = sums[0][8:9, LANES : LANES + side]
    gain[:, side:] = sums[1][8:9, LANES : LANES + side]


def parameters(parts, channels, width):
    total, columns = parts[0].shape
    at = total // BELOW - 1

    def whole(shape):
        return pl.BlockSpec(shape, lambda i: (0, 0))

    shapes = [(8, channels), (8, LANES), (1, width)]
    return pl.pallas_call(
        lambda *refs: parameter_kernel(width // 2, *refs),
        grid=(1,),
        in_specs=[pl.BlockSpec((BELOW, columns), lambda i: (at, 0))] * len(parts),
        out_specs=[whole(shape) for shape in shapes],
        out_shape=[jax.ShapeDtypeStruct(shape, f32) for shape in shapes],
        compiler_params=pltpu.CompilerParams(vmem_limit_bytes=VMEM),
        cost_estimate=pl.CostEstimate(flops=1_000_000, bytes_accessed=1_000_000, transcendentals=0),
        name="parameters",
    )(*parts)


def assemble_kernel(place, *refs):
    parts, out = refs[:-1], refs[-1]
    chips = len(parts) // 2
    rows = parts[0].shape[0] - BELOW
    for k in range(2):
        for j in range(chips):
            at = pl.multiple_of((k * chips + (place[0] ^ j)) * rows, BELOW)
            out[pl.ds(at, rows), :] = parts[k * chips + j][0:rows, :]


def assembled(place, parts):
    vmem = pl.BlockSpec(memory_space=pltpu.VMEM)
    rows, columns = parts[0].shape
    return pl.pallas_call(
        assemble_kernel,
        in_specs=[pl.BlockSpec(memory_space=pltpu.SMEM)] + [vmem] * len(parts),
        out_specs=vmem,
        out_shape=jax.ShapeDtypeStruct(((rows - BELOW) * len(parts), columns), bf16),
        compiler_params=pltpu.CompilerParams(vmem_limit_bytes=VMEM),
        cost_estimate=pl.CostEstimate(flops=1_000_000, bytes_accessed=1_000_000, transcendentals=0),
        name="assembled",
    )(place, *parts)


def split_kernel(ranks, core, tokens, mine, sent):
    batch, piece, width = tokens.shape
    half = batch // 2
    rows = width // ranks
    first = core[0] == 0
    for b in range(batch):
        parts = [
            jnp.concatenate(
                [
                    tokens[b, :, c * rows : (c + 1) * rows].astype(f32)
                    for c in range(k, ranks, 2)
                ],
                axis=1,
            )
            for k in range(2)
        ]
        own = jnp.where(first, parts[0], parts[1])
        other = jnp.where(first, parts[1], parts[0])
        here = first if b < half else jnp.logical_not(first)

        @pl.when(here)
        def _():
            mine[b % half] = jnp.concatenate([own, other], axis=1).astype(bf16)

        @pl.when(jnp.logical_not(here))
        def _():
            sent[b % half] = jnp.concatenate([other, own], axis=1).astype(bf16)


def split_tokens(core, tokens, ranks):
    batch, piece, width = tokens.shape
    vmem = pl.BlockSpec(memory_space=pltpu.VMEM)
    shape = jax.ShapeDtypeStruct((batch // 2, piece, width), bf16)
    return pl.pallas_call(
        lambda *refs: split_kernel(ranks, *refs),
        in_specs=[pl.BlockSpec(memory_space=pltpu.SMEM), vmem],
        out_specs=[vmem, vmem],
        out_shape=[shape, shape],
        compiler_params=pltpu.CompilerParams(vmem_limit_bytes=VMEM),
        cost_estimate=pl.CostEstimate(flops=1_000_000, bytes_accessed=1_000_000, transcendentals=0),
        name="split_tokens",
    )(core, tokens)


def distinct(pieces):
    arrays, where = [], []
    for array, index in pieces:
        found = [k for k, a in enumerate(arrays) if a is array]
        if not found:
            arrays.append(array)
            found = [len(arrays) - 1]
        where.append((found[0], index))
    return arrays, where


def rows_call(kernel, pieces, extra, name):
    arrays, where = distinct(pieces)
    vmem = pl.BlockSpec(memory_space=pltpu.VMEM)
    rows, width = arrays[0].shape[1:]
    return pl.pallas_call(
        lambda *refs: kernel(where, *refs),
        in_specs=[vmem] * (len(arrays) + len(extra)),
        out_specs=vmem,
        out_shape=jax.ShapeDtypeStruct((rows * len(where), width), bf16),
        compiler_params=pltpu.CompilerParams(vmem_limit_bytes=VMEM),
        cost_estimate=pl.CostEstimate(flops=1_000_000, bytes_accessed=1_000_000, transcendentals=0),
        name=name,
    )(*extra, *arrays)


def project_kernel(where, gain, columns, *refs):
    pieces, (out, projected) = refs[:-2], refs[-2:]
    rows = pieces[0].shape[1]

    @pl.when(pl.program_id(0) == 0)
    def _():
        for k, (a, index) in enumerate(where):
            values = pieces[a][index].astype(f32)
            scale = lax.rsqrt(jnp.mean(values * values, axis=1, keepdims=True) + EPSILON)
            out[k * rows : (k + 1) * rows, :] = (values * scale * gain[...]).astype(bf16)

    tile = 256
    for k in range(out.shape[0] // tile):
        at = slice(k * tile, (k + 1) * tile)
        projected[at, :] = dot(out[at, :], columns[...])


def project(pieces, gain, columns):
    arrays, where = distinct(pieces)
    rows, width = arrays[0].shape[1:]
    length, wide = rows * len(where), columns.shape[1]
    tile = 384 if wide % 384 == 0 else LANES

    def whole(shape):
        return pl.BlockSpec(shape, lambda i: (0,) * len(shape))

    return pl.pallas_call(
        lambda *refs: project_kernel(where, *refs),
        grid=(wide // tile,),
        in_specs=[whole(gain.shape), pl.BlockSpec((width, tile), lambda i: (0, i))]
        + [whole(a.shape) for a in arrays],
        out_specs=[whole((length, width)), pl.BlockSpec((length, tile), lambda i: (0, i))],
        out_shape=[
            jax.ShapeDtypeStruct((length, width), bf16),
            jax.ShapeDtypeStruct((length, wide), f32),
        ],
        compiler_params=pltpu.CompilerParams(vmem_limit_bytes=VMEM),
        cost_estimate=pl.CostEstimate(flops=1_000_000, bytes_accessed=1_000_000, transcendentals=0),
        name="project",
    )(gain, columns, *arrays)


def joined_kernel(where, *refs):
    pieces, out = refs[:-1], refs[-1]
    rows = pieces[0].shape[1]
    for k, (a, index) in enumerate(where):
        out[k * rows : (k + 1) * rows, :] = pieces[a][index]


def joined_rows(pieces):
    return rows_call(joined_kernel, pieces, [], "joined_rows")


def gate_kernel(result, projected, g_mixed, norms, by_channel, g_result, g_gate, mixed):
    local = result.shape[1]
    gain = by_channel[5:6, 0:local]
    r = norms[:, 0:1]
    y = result[...]
    gate = projected[...]
    gate_s = sigmoid(gate)
    silu = gate * gate_s
    gated = y * silu
    mixed[...] = (gated * r * gain).astype(bf16)
    g_gated = r * gain * g_mixed[...] - gated * norms[:, 1:2]
    g_result[...] = (g_gated * silu).astype(bf16)
    g_gate[...] = (g_gated * y * gate_s * (1.0 + gate * (1.0 - gate_s))).astype(bf16)


def gate_gradients(result, projected, g_mixed, norms, by_channel):
    length, local = result.shape
    width = 256

    def here(i):
        return (i, 0)

    block = pl.BlockSpec((width, local), here)
    return pl.pallas_call(
        gate_kernel,
        grid=(length // width,),
        in_specs=[
            block,
            block,
            block,
            pl.BlockSpec((width, 2), here),
            pl.BlockSpec(by_channel.shape, lambda i: (0, 0)),
        ],
        out_specs=[block] * 3,
        out_shape=[jax.ShapeDtypeStruct((length, local), bf16)] * 3,
        compiler_params=pltpu.CompilerParams(vmem_limit_bytes=VMEM),
        cost_estimate=pl.CostEstimate(flops=1_000_000, bytes_accessed=1_000_000, transcendentals=0),
        name="gate_gradients",
    )(result, projected, g_mixed, norms, by_channel)


def output_kernel(core, tokens, kept, got, output):
    batch = tokens.shape[0]
    half = batch // 2
    for b in range(batch):
        mine = core[0] == b // half
        total = jnp.where(mine, kept[b % half], got[b % half].astype(f32))
        output[b] = (tokens[b].astype(f32) + total).astype(bf16)


def token_kernel(ranks, core, tokens, cotangent, gain, kept, got, gradient):
    batch, _, width = tokens.shape
    half, side, rows = batch // 2, width // 2, width // ranks
    gains = (gain[:, :side], gain[:, side:])
    first = core[0] == 0
    gains = (jnp.where(first, gains[0], gains[1]), jnp.where(first, gains[1], gains[0]))
    for b in range(batch):
        owner = b // half
        g = jnp.where(core[0] == owner, kept[b % half], got[b % half].astype(f32))
        parts = (g[:, :side], g[:, side:]) if owner == 0 else (g[:, side:], g[:, :side])
        parts = (parts[0] * gains[0], parts[1] * gains[1])
        weighted = jnp.concatenate(
            [part[:, c * rows : (c + 1) * rows] for c in range(ranks // 2) for part in parts],
            axis=1,
        )
        values = tokens[b].astype(f32)
        scale = lax.rsqrt(jnp.mean(values * values, axis=1, keepdims=True) + EPSILON)
        inner = jnp.mean(values * weighted, axis=1, keepdims=True)
        gradient[b] = (
            cotangent[b].astype(f32) + scale * weighted - values * (scale * scale * scale * inner)
        )


def share_kernel(chips, place, summed, *parts):
    share, columns = parts[0].shape
    width = summed.shape[1]
    for j in range(chips):
        c = place[0] ^ j
        for k in range(columns // width):
            at = pl.multiple_of((k * chips + c) * share, share)
            parts[j][:, k * width : (k + 1) * width] = summed[pl.ds(at, share), :]


def shares_by_chip(place, summed, chips, share, columns):
    vmem = pl.BlockSpec(memory_space=pltpu.VMEM)
    return pl.pallas_call(
        lambda *refs: share_kernel(chips, *refs),
        in_specs=[pl.BlockSpec(memory_space=pltpu.SMEM), vmem],
        out_specs=[vmem] * chips,
        out_shape=[jax.ShapeDtypeStruct((share, columns), bf16)] * chips,
        compiler_params=pltpu.CompilerParams(vmem_limit_bytes=VMEM),
        cost_estimate=pl.CostEstimate(flops=1_000_000, bytes_accessed=1_000_000, transcendentals=0),
        name="shares_by_chip",
    )(place, summed)


def early_kernel(across, place, summed, *refs):
    parts, out = refs[:-1], refs[-1]
    share, local = parts[0].shape
    chips = len(parts)
    inner = chips * local
    for j, part in enumerate(parts):
        out[:, pl.ds(pl.multiple_of((place[0] ^ j) * local, LANES), local)] = part[...]
    rounds = (summed.shape[0] // share - chips) // across
    for k in range(across):
        for r in range(rounds):
            start = chips * share + (k * rounds + r) * share
            to = inner + (r * across + k) * local
            out[:, to : to + local] = summed[start : start + share, :]


def late_kernel(heads, place, *refs):
    parts, out = refs[:-1], refs[-1]
    chips = len(parts)
    each = heads // chips
    columns = parts[0].shape[1]
    local = columns - 2 * N - LANES
    inner = chips * local
    row = lax.broadcasted_iota(jnp.int32, (LANES, heads), 0)
    lane = lax.broadcasted_iota(jnp.int32, (LANES, heads), 1)
    steps = jnp.zeros((out.shape[0], heads), f32)
    shared = jnp.zeros((out.shape[0], 2 * N), f32)
    for j, part in enumerate(parts):
        c = place[0] ^ j
        out[:, pl.ds(pl.multiple_of(c * local, LANES), local)] = part[:, 0:local]
        shared = shared + part[:, local : local + 2 * N].astype(f32)
        pick = jnp.logical_and(lane == c * each + row, row < each)
        steps = steps + dot(part[:, local + 2 * N :], jnp.where(pick, 1.0, 0.0).astype(bf16))
    out[:, inner : inner + 2 * N] = shared.astype(bf16)
    out[:, inner + 2 * N :] = steps.astype(bf16)


def joined_shares(kernel, place, arrays, shape, name):
    vmem = pl.BlockSpec(memory_space=pltpu.VMEM)
    return pl.pallas_call(
        kernel,
        in_specs=[pl.BlockSpec(memory_space=pltpu.SMEM)] + [vmem] * len(arrays),
        out_specs=vmem,
        out_shape=jax.ShapeDtypeStruct(shape, bf16),
        compiler_params=pltpu.CompilerParams(vmem_limit_bytes=VMEM),
        cost_estimate=pl.CostEstimate(flops=1_000_000, bytes_accessed=1_000_000, transcendentals=0),
        name=name,
    )(place, *arrays)


def weights_kernel(early, rest, in_weight, step_weight, total_in, total_step, by_gain):
    inner = in_weight.shape[1] - 2 * N - early_columns(in_weight)
    heads = step_weight.shape[1]
    first = early[:, 0:inner].astype(f32)
    last = rest[:, 0 : inner + 2 * N].astype(f32)
    step = rest[:, inner + 2 * N :].astype(f32)
    total_in[:, 0:inner] = first
    total_in[:, inner:] = last
    total_step[...] = step
    by_gain[...] = (
        jnp.sum(in_weight[:, 0:inner].astype(f32) * first, axis=1, keepdims=True)
        + jnp.sum(in_weight[:, inner:].astype(f32) * last, axis=1, keepdims=True)
        + jnp.sum(step_weight[...].astype(f32) * step, axis=1, keepdims=True)
    )


def early_columns(in_weight):
    return (in_weight.shape[1] - 2 * N) // 2


def weight_totals(early, rest, in_weight, step_weight):
    rows = in_weight.shape[0]
    block = rows // 4 if rows % 64 == 0 else rows

    def here(i):
        return (i, 0)

    arrays = [early, rest, in_weight, step_weight]
    widths = [in_weight.shape[1], step_weight.shape[1], 1]
    return pl.pallas_call(
        weights_kernel,
        grid=(rows // block,),
        in_specs=[pl.BlockSpec((block, a.shape[1]), here) for a in arrays],
        out_specs=[pl.BlockSpec((block, width), here) for width in widths],
        out_shape=[jax.ShapeDtypeStruct((rows, width), f32) for width in widths],
        compiler_params=pltpu.CompilerParams(vmem_limit_bytes=VMEM),
        cost_estimate=pl.CostEstimate(flops=1_000_000, bytes_accessed=1_000_000, transcendentals=0),
        name="weight_totals",
    )(*arrays)


def whole_call(kernel, scalar, arrays, shape, dtype, name):
    vmem = pl.BlockSpec(memory_space=pltpu.VMEM)
    return pl.pallas_call(
        kernel,
        in_specs=[pl.BlockSpec(memory_space=pltpu.SMEM)] + [vmem] * len(arrays),
        out_specs=vmem,
        out_shape=jax.ShapeDtypeStruct(shape, dtype),
        compiler_params=pltpu.CompilerParams(vmem_limit_bytes=VMEM),
        cost_estimate=pl.CostEstimate(flops=1_000_000, bytes_accessed=1_000_000, transcendentals=0),
        name=name,
    )(scalar, *arrays)


def across_chips(x, bit):
    return lax.ppermute(x, "chip", [(i, i ^ bit) for i in range(lax.axis_size("chip"))])


def sibling(x):
    return lax.ppermute(x, "core", [(0, 1), (1, 0)])


def chip_bits(turn):
    chips = lax.axis_size("chip")
    bits = [1 << k for k in range(chips.bit_length() - 1)]
    return bits if turn == 0 else bits[::-1]


def after(x, *deps):
    return lax.optimization_barrier((x, deps))[0]


class Gather:
    def __init__(self, block):
        self.own = {bit: across_chips(block, bit) for bit in chip_bits(0)}
        self.have = []
        for turn in range(2):
            have = {0: (block, turn)}
            for bit in chip_bits(turn)[:1]:
                have[bit] = (self.own[bit], turn)
            self.have.append(have)

    def received(self):
        return list(self.own.values())

    def relay(self, *deps):
        relayed = []
        for turn, have in enumerate(self.have):
            for bit in chip_bits(turn)[1:]:
                new = {bit: (self.own[bit], turn)}
                for j, (array, index) in sorted(have.items()):
                    if j:
                        part = array[index : index + 1]
                        part = after(part, *deps) if deps else part
                        relayed.append(part)
                        new[j ^ bit] = (across_chips(part, bit), 0)
                have.update(new)
        return relayed

    def slots(self):
        return [self.have[turn][j] for turn, j in slot_order(len(self.have[0]))]


class Scatter:
    def __init__(self, rows, chips, *deps, keep_rows=None):
        self.rows = keep_rows or rows
        self.bits = [chip_bits(turn)[::-1] for turn in range(2)]
        gives = tuple(part.astype(bf16) for part in rows(True))
        self.gives = after(gives, *deps) if deps else gives
        self.kept = None
        self.sent = [across_chips(x, bits[0]) for x, bits in zip(self.gives, self.bits)]

    def step(self, *deps):
        kept = self.rows(False) if self.kept is None else self.kept
        sent = after(tuple(self.sent), *deps) if deps else self.sent
        self.kept, self.sent = [], []
        for turn, bits in enumerate(self.bits):
            bits.pop(0)
            total = kept[turn].astype(f32) + sent[turn].astype(f32)
            if bits:
                half = total.shape[0] // 2
                self.kept.append(total[:half])
                self.sent.append(across_chips(total[half:].astype(bf16), bits[0]))
            else:
                self.kept.append(total)

    def done(self, *deps):
        while self.bits[0]:
            self.step(*deps)
        return [part[0] for part in self.kept]


def chip_total(x):
    order = slot_order(x.shape[-2] // 2)
    for bit in chip_bits(0):
        moved = [order.index((turn, j ^ bit)) for turn, j in order]
        pick = jnp.asarray([[float(m == k) for k in range(len(order))] for m in moved], f32)
        x = x + jnp.einsum("st,atp->asp", pick, across_chips(x, bit), precision=precise)
    return x


def across_groups(x, step):
    return lax.ppermute(x, "dp", [(i, i ^ step) for i in range(lax.axis_size("dp"))])


def by_group(x):
    blocks, rows, width = x.shape
    count = lax.axis_size("dp")
    return x.reshape(blocks, count, rows // count, width).transpose(1, 0, 2, 3)


def group_scatter(x):
    return lax.psum_scatter(x, "dp", scatter_dimension=0, tiled=False)


def group_gather(x):
    return lax.all_gather(x, "dp", axis=0, tiled=True)


def body(
    tokens,
    norm_gain,
    in_weight,
    step_weight,
    filter_weight,
    filter_bias,
    step_bias,
    log_rate,
    skip_scale,
    inner_gain,
    out_weight,
    cotangent,
):
    chips = lax.axis_size("chip")
    chip, core = lax.axis_index("chip"), lax.axis_index("core")
    rank = chip * 2 + core
    batch, piece, width = tokens.shape
    half = batch // 2
    ranks = chips * 2
    heads = log_rate.shape[0] * ranks
    inner = inner_gain.shape[0] * ranks
    local_heads, local = heads // chips, inner // chips
    rows = in_weight.shape[0]
    side = width // 2
    taps = filter_weight.shape[0]
    channels = local + 2 * N
    first = core == 0

    def own_first(a, b):
        return (jnp.where(first, a, b), jnp.where(first, b, a))

    columns_in = 2 * local + 2 * N + LANES
    place = jnp.stack([chip, core]).astype(jnp.int32)
    per_head = jnp.stack([step_bias, log_rate, skip_scale])
    per_head = jnp.pad(per_head, ((0, 5), (0, 0)))
    packed_weight = pack_columns(
        place,
        [
            in_weight,
            step_weight,
            filter_weight,
            filter_bias[None],
            inner_gain[None],
            norm_gain[None],
        ],
        per_head,
        chips,
        columns_in,
        inner,
    )

    def of_core(a, which):
        return lax.dynamic_slice_in_dim(a, which * half, half, 0)

    core_ref = core.astype(jnp.int32).reshape(1)
    mine, sent = split_tokens(after(core_ref, *packed_weight), tokens, ranks)
    got = sibling(sent)
    token_blocks = [jnp.stack([mine[b], got[b]]) for b in range(half)]
    mine_cot, got_cot = of_core(cotangent, core), sibling(of_core(cotangent, 1 - core))
    cot_blocks = [jnp.stack([mine_cot[b], got_cot[b]]) for b in range(half)]

    parts = [across_chips(part, j) if j else part for j, part in enumerate(packed_weight)]
    parts = parts + [sibling(part) for part in parts]
    by_channel, by_head, gain = parameters(parts, channels, width)
    columns = assembled(place, parts)
    out_low, out_high = own_first(out_weight, sibling(out_weight))
    out_rows = jnp.concatenate([out_low, out_high], axis=0)

    def tn(a, b):
        return lax.dot_general(a, b, (((0,), (0,)), ((), ())), preferred_element_type=f32)

    rank_ref = rank.astype(jnp.int32).reshape(1)
    spans = range(half)
    queue = [Gather(token_blocks[0])]
    for block in token_blocks[1:] + cot_blocks:
        queue.append((block, None))
    moved = 0

    def advance(*deps):
        nonlocal moved
        if moved >= len(queue):
            return []
        now = queue[moved]
        before = [part for part, _ in queue[moved - 1].slots()] if moved else []
        relayed = now.relay(*deps, *before)
        moved += 1
        if moved < len(queue):
            waits = now.received() if moved > 1 else [part for part, _ in now.slots()]
            block = after(queue[moved][0], *waits, *deps)
            queue[moved] = Gather(block)
            relayed = relayed + [block]
        return relayed

    def slot_rows(a, run):
        count = a.shape[0] // 2

        def rows(upper):
            part = run(a[:count] if upper else a[count:])
            return part.reshape(2, chips // 2, piece, width)

        return rows

    advance()
    normed, projected, fronts = [], [], []
    for b in spans:
        ready = after(gain, fronts[b - 1][2]) if b else gain
        normed_b, projected_b = project(queue[b].slots(), ready, columns)
        normed.append(normed_b)
        projected.append(projected_b)
        issued = advance(*([projected[0]] if b == 0 else []))
        fronts.append(
            scan_forward(
                rank_ref, projected[b], by_channel, after(by_head, *issued), local, piece
            )
        )
        if b + 1 < half:
            advance(fronts[b][2])
    while moved < len(queue):
        advance(fronts[-1][2])
    cots = queue[half:]

    all_cot, g_mixed, stats, local_stats = [], [], [], []
    for b in spans:
        result, scaled, squares, states = fronts[b]
        all_cot.append(joined_rows(cots[b].slots()))
        g_mixed.append(dot_nt(all_cot[b], out_rows))
        both = jnp.stack([squares[:, 0], jnp.sum(scaled.astype(f32) * g_mixed[b], axis=1)])
        local_stats.append(both)
        stats.append(chip_total(both.reshape(2, ranks, piece)).reshape(both.shape) / inner)
    g_results, g_gates, mixed, outs = [], [], [], []
    for b in spans:
        r = lax.rsqrt(stats[b][0] + EPSILON)
        norms = jnp.stack([r, r * r * r * stats[b][1]], axis=1)
        if b + 1 < half:
            norms = after(norms, local_stats[b + 1])
        g_result, g_gate, mixed_b = gate_gradients(
            fronts[b][0], projected[b], g_mixed[b], norms, by_channel
        )
        g_results.append(g_result)
        g_gates.append(g_gate)
        mixed.append(mixed_b)
        outs.append(Scatter(slot_rows(mixed_b, lambda x: dot(x, out_rows)), chips, stats[-1]))

    def row_sums(parts):
        far = [tn(normed[b][:, side:], parts[b]) for b in range(len(parts))]
        near = [tn(normed[b][:, :side], parts[b]) for b in range(len(parts))]
        return far, near

    def core_sum(far, near, *deps):
        sent = after(sum(far).astype(bf16), *deps)
        total = (sum(near) + sibling(sent).astype(f32)).astype(bf16)
        return total.reshape(chips, rows, -1)

    def by_chip(near):
        found = []
        for j in range(chips):
            part = lax.dynamic_index_in_dim(near, chip ^ j, 0, keepdims=True)
            found.append(across_chips(part, j) if j else part)
        return found

    def exchanged(parts):
        return [across_chips(part, j) if j else part for j, part in enumerate(parts)]

    def in_place(parts, size, total):
        whole = jnp.zeros(parts[0].shape[:2] + (total,), bf16)
        for j, part in enumerate(parts):
            whole = lax.dynamic_update_slice_in_dim(whole, part[:, :, :size], (chip ^ j) * size, 2)
        return whole

    gate_near = core_sum(*row_sums(g_gates))
    out_gradient = sum(tn(mixed[b], all_cot[b]) for b in spans)
    out_near, out_far = own_first(out_gradient[: local // 2], out_gradient[local // 2 :])
    out_near = (out_near + sibling(out_far.astype(bf16)).astype(f32)).astype(bf16)
    groups = lax.axis_size("dp")
    share = rows // groups
    out_near = out_near.reshape(groups, -1, width)
    out_near = jnp.concatenate(
        [out_near[:, :, k : k + local] for k in range(0, width, local)], axis=1
    )
    gate_near = by_group(gate_near).reshape(groups, -1, local)
    early = group_scatter(jnp.concatenate([gate_near, out_near], axis=1))

    g_columns, sums, g_normed, far, near = [], [], [], [], []
    ready = after(by_head, gate_near, out_near, *[x for out in outs for x in out.gives])
    for b in spans:
        g_proj, sum_channel, sum_head = scan_backward(
            rank_ref, projected[b], g_results[b], g_gates[b], fronts[b][3], by_channel, ready, piece
        )
        g_columns.append(g_proj)
        sums.append((sum_channel, sum_head))
        waits = [sum_head]
        for part in outs if b == 0 else []:
            part.step(sum_head)
        rest = g_proj[:, local:]
        far.append(tn(normed[b][:, side:], rest))
        if b == half - 1:
            g_proj = after(g_proj, early)
            rest = g_proj[:, local:]
        near.append(tn(normed[b][:, :side], rest))
        if b == 0:
            early = after(early, sum_head)
        if b == half - 1:
            rest_near = core_sum(far, near)
            sums[-1] = after(sums[-1], rest_near)
        send = slot_rows(g_proj, lambda x: dot_nt(x, columns))
        late = after(g_proj, rest_near) if b == half - 1 else g_proj
        keep = slot_rows(late, lambda x: dot_nt(x, columns))
        g_normed.append(Scatter(send, chips, *([early] if b == 0 else []), keep_rows=keep))
        if b == 0:
            if share % 16 == 0:
                gate_parts = exchanged(shares_by_chip(place, early, chips, share, local))
                early = joined_shares(
                    lambda *refs: early_kernel(width // local, *refs),
                    place,
                    [early, *gate_parts],
                    (share, 2 * inner),
                    "early_share",
                )
            else:
                gate_parts = by_chip(early[: chips * share].reshape(chips, share, local))
                out_share = jnp.split(early[chips * share :], width // local)
                out_share = jnp.concatenate(out_share, axis=1)
                early = [in_place(gate_parts, local, inner)[0]]
                early = early + jnp.split(out_share, inner // width)
                early = jnp.concatenate(early, axis=1)
            waits = [early]
            early = group_gather(early)
        ready = after(by_head, far[b], near[b], *g_normed[b].gives, *waits)
    early = after(early, rest_near)
    total_out = early[:, inner:].reshape(groups, share, -1, width)
    total_out = total_out.transpose(0, 2, 1, 3).reshape(-1, width)
    late_columns = 2 * N + LANES
    rest_blocks = by_group(rest_near).reshape(groups, -1, local + late_columns)
    if local % late_columns == 0:
        cuts = range(0, local + late_columns, late_columns)
        rest_blocks = [rest_blocks[:, :, k : k + late_columns] for k in cuts]
        rest_sum = group_scatter(jnp.concatenate(rest_blocks, axis=1))
    else:
        cuts = [0]
        rest_sum = group_scatter(rest_blocks)
    if share % 16 == 0:
        rest_parts = shares_by_chip(place, rest_sum, chips, share, local + late_columns)
        rest_total = joined_shares(
            lambda *refs: late_kernel(heads, *refs),
            place,
            exchanged(rest_parts),
            (share, inner + 2 * N + heads),
            "late_share",
        )
    else:
        rest_sum = jnp.concatenate(jnp.split(rest_sum, len(cuts)), axis=1)
        rest_parts = by_chip(rest_sum.reshape(chips, share, -1))
        shared = sum(part[:, :, local : local + 2 * N].astype(f32) for part in rest_parts)
        step_parts = [part[:, :, local + 2 * N :] for part in rest_parts]
        rest_total = jnp.concatenate(
            [
                in_place(rest_parts, local, inner),
                shared.astype(bf16),
                in_place(step_parts, local_heads, heads),
            ],
            axis=2,
        )[0]
    late = rest_total
    rest_total = group_gather(rest_total)
    total_out = total_out.astype(f32)

    total_in, total_step, total_gain = weight_totals(early, rest_total, in_weight, step_weight)
    total_gain = total_gain[:, 0] / norm_gain.astype(f32)
    total_inner = jnp.sum(out_weight.astype(f32) * total_out, axis=1) / inner_gain.astype(f32)

    def regrouped(parts):
        kept = jnp.stack([part[0] for part in parts])
        got = sibling(jnp.stack([part[1] for part in parts]).astype(bf16))
        return (kept, got)

    out_sums = [out.done(rest_near) for out in outs]
    g_normed = [part.done(rest_near) for part in g_normed]

    sum_channel = sum(part[0] for part in sums)
    sum_head = sum(part[1] for part in sums)

    def placed(a, size):
        empty = jnp.zeros((a.shape[0], size), f32)
        return lax.dynamic_update_slice_in_dim(empty, a, chip * a.shape[1], 1)

    skip = jnp.sum(sum_channel[5, :local].reshape(local_heads, HEAD), axis=1)[None]
    packed = jnp.concatenate(
        [
            jnp.concatenate(
                [placed(sum_channel[: taps + 1, :local], inner), sum_channel[: taps + 1, local:]],
                axis=1,
            ).reshape(-1),
            placed(jnp.concatenate([sum_head[:2, :local_heads], skip], axis=0), heads).reshape(-1),
        ]
    )
    packed = jnp.pad(packed, (0, -packed.shape[0] % 1024)).reshape(-1, LANES)
    packed = after(packed, rest_near)
    packed = packed + sibling(packed)
    for bit in chip_bits(0):
        packed = packed + across_chips(packed, bit)
    for bit in [1 << k for k in range(lax.axis_size("dp").bit_length() - 1)]:
        packed = packed + across_groups(packed, bit)
    packed = after(packed, late).reshape(-1)
    cut = (taps + 1) * (inner + 2 * N)

    def own_of(a):
        size = a.shape[1] // ranks
        return lax.dynamic_slice_in_dim(a, rank * size, size, 1)

    channel_totals = own_of(packed[:cut].reshape(taps + 1, -1))
    head_totals = own_of(packed[cut : cut + 3 * heads].reshape(3, heads))

    kept, got = regrouped(out_sums)
    output = whole_call(output_kernel, core_ref, [tokens, kept, got], tokens.shape, bf16, "output")
    kept, got = regrouped(g_normed)
    token_gradient = whole_call(
        lambda *refs: token_kernel(ranks, *refs),
        core_ref,
        [tokens, cotangent, gain, kept, got],
        tokens.shape,
        f32,
        "token_gradient",
    )
    return (
        output,
        token_gradient,
        total_gain,
        total_in,
        total_step,
        channel_totals[:taps],
        channel_totals[taps],
        head_totals[0],
        head_totals[1],
        head_totals[2],
        total_inner,
        total_out,
    )


def solution(mesh):
    ranks, groups = mesh.shape["sp"], mesh.shape["dp"]
    fine = Mesh(mesh.devices.reshape(ranks // 2, 2, groups), ("chip", "core", "dp"))
    sp = ("chip", "core")
    return jax.shard_map(
        body,
        mesh=fine,
        in_specs=(
            P("dp", sp, None),
            P(sp),
            P(sp, None),
            P(sp, None),
            P(None, sp),
            P(sp),
            P(sp),
            P(sp),
            P(sp),
            P(sp),
            P(sp, None),
            P("dp", sp, None),
        ),
        out_specs=(
            P("dp", sp, None),
            P("dp", sp, None),
            P(sp),
            P(sp, None),
            P(sp, None),
            P(None, sp),
            P(sp),
            P(sp),
            P(sp),
            P(sp),
            P(sp),
            P(sp, None),
        ),
        check_vma=False,
    )
```

```python
import jax
import jax.numpy as jnp
from jax import lax
from jax.experimental import pallas as pl
from jax.experimental.pallas import tpu as pltpu
from jax.sharding import Mesh, PartitionSpec as P

N = 128
HEAD = 64
LANES = 128
VMEM = 32 * 1024 * 1024
EPSILON = 1e-05
f32, bf16 = jnp.float32, jnp.bfloat16
precise = lax.Precision.HIGHEST


def sigmoid(v):
    return 0.5 * jnp.tanh(0.5 * v) + 0.5


def dot(a, b):
    return jnp.dot(a, b, preferred_element_type=f32)


def dot_nt(a, b):
    return lax.dot_general(a, b, (((1,), (1,)), ((), ())), preferred_element_type=f32)


def spread_pair(low, a, p):
    return jnp.where(low, a[:, 2 * p : 2 * p + 1], a[:, 2 * p + 1 : 2 * p + 2])


def stacked(low, a):
    zero = jnp.zeros_like(a)
    return jnp.concatenate([jnp.where(low, a, zero), jnp.where(low, zero, a)], axis=0).astype(bf16)


def running_sum(x):
    rows = lax.broadcasted_iota(jnp.int32, x.shape, 0)
    k = 1
    while k < x.shape[0]:
        x = x + jnp.where(rows >= k, pltpu.roll(x, k, 0), 0.0)
        k *= 2
    return x


def forward_kernel(
    rank, projected, by_channel, by_head, result, scaled, squares, states, state, window
):
    step = pl.program_id(0)
    width, local = result.shape
    channels = local + 2 * N
    taps = 4

    @pl.when(step == 0)
    def _():
        state[...] = jnp.zeros_like(state)
        window[0:8, :] = jnp.zeros((8, channels), f32)

    @pl.when(step > 0)
    def _():
        window[0:8, :] = window[width : width + 8, :]

    window[8 : 8 + width, :] = projected[:, local : local + channels]
    filtered = by_channel[4:5, :]
    for tap in range(taps):
        at = 9 - taps + tap
        filtered = filtered + by_channel[tap : tap + 1, :] * window[at : at + width, :]
    active = filtered * sigmoid(filtered)
    entry = active[:, local : local + N]
    readout = active[:, local + N :].astype(bf16)
    steps = jax.nn.softplus(projected[:, local + channels :] + by_head[0:1, :])
    rows = lax.broadcasted_iota(jnp.int32, (width, width), 0)
    cols = lax.broadcasted_iota(jnp.int32, (width, width), 1)
    running = running_sum(steps * by_head[1:2, :])
    across = running.T
    meeting = jnp.where(cols <= rows, dot_nt(readout, entry.astype(bf16)), 0.0)
    before = state[...].astype(bf16)
    states[0] = before
    carried = dot(readout, before)
    entry_t = entry.T.astype(bf16)
    low = lax.broadcasted_iota(jnp.int32, (width, LANES), 1) < HEAD
    total = jnp.zeros((width, LANES), f32)
    weighted, decay = [], []
    for p in range(local // LANES):
        at = slice(p * LANES, (p + 1) * LANES)
        signal = active[:, at]
        mixing, along = [], []
        for h in (2 * p, 2 * p + 1):
            along.append(jnp.broadcast_to(running[:, h : h + 1], (width, width)))
            span = jnp.minimum(along[-1] - across[h : h + 1, :], 0.0)
            mixing.append((jnp.exp(span) * meeting).astype(bf16))
        entered = signal * spread_pair(low, steps, p)
        y = dot(jnp.concatenate(mixing, axis=1), stacked(low, entered))
        along = jnp.where(low, along[0], along[1])
        grown_p = jnp.exp(along)
        y = y + grown_p * carried[:, at] + by_channel[6:7, at] * signal
        result[:, at] = y
        gate = projected[:, at]
        gated = y * gate * sigmoid(gate)
        scaled[:, at] = (gated * by_channel[5:6, at]).astype(bf16)
        total = total + gated * gated
        weighted.append((entered * jnp.exp(along[width - 1 : width, :] - along)).astype(bf16))
        decay.append(grown_p[width - 1 : width, :])
    squares[...] = jnp.sum(total, axis=1, keepdims=True)
    state[...] = jnp.concatenate(decay, axis=1) * state[...] + dot(
        entry_t, jnp.concatenate(weighted, axis=1)
    )


def backward_kernel(
    rank,
    projected,
    tail,
    g_result,
    g_gate,
    states,
    by_channel,
    by_head,
    g_projected,
    sum_channel,
    sum_head,
    adjoint,
    window,
    ahead,
):
    step = pl.program_id(0)
    last = pl.num_programs(0) - 1
    width, local = g_result.shape
    channels = local + 2 * N
    taps = 4

    @pl.when(step == 0)
    def _():
        adjoint[...] = jnp.zeros_like(adjoint)
        ahead[width : width + 8, :] = jnp.zeros((8, channels), f32)
        sum_channel[...] = jnp.zeros_like(sum_channel)
        sum_head[...] = jnp.zeros_like(sum_head)

    @pl.when(step > 0)
    def _():
        ahead[width : width + 8, :] = ahead[0:8, :]

    window[0:8, :] = jnp.where(step == last, 0.0, tail[:, local : local + channels])
    window[8 : 8 + width, :] = projected[:, local : local + channels]
    filtered = by_channel[4:5, :]
    for tap in range(taps):
        at = 9 - taps + tap
        filtered = filtered + by_channel[tap : tap + 1, :] * window[at : at + width, :]
    gate_f = sigmoid(filtered)
    active = filtered * gate_f
    slope = gate_f * (1.0 + filtered * (1.0 - gate_f))
    entry = active[:, local : local + N]
    readout = active[:, local + N :]
    entry_b, readout_b = entry.astype(bf16), readout.astype(bf16)
    shifted = projected[:, local + channels :] + by_head[0:1, :]
    steps = jax.nn.softplus(shifted)
    rate = by_head[1:2, :]
    rows = lax.broadcasted_iota(jnp.int32, (width, width), 0)
    cols = lax.broadcasted_iota(jnp.int32, (width, width), 1)
    falls = steps * rate
    running = running_sum(falls)
    across = running.T
    meeting = jnp.where(rows <= cols, dot_nt(entry_b, readout_b), 0.0)
    before = states[0]
    after = adjoint[...].astype(bf16)
    carried = dot(readout_b, before)
    returned = dot(entry_b, after)
    readout_t = readout.T.astype(bf16)
    lane = lax.broadcasted_iota(jnp.int32, (width, LANES), 1)
    low = lane < HEAD
    g_projected[:, 0:local] = g_gate[...]
    ones = jnp.ones((width, LANES), bf16)
    by_col = jnp.zeros((width, LANES), f32)
    pick_rows = lax.broadcasted_iota(jnp.int32, (LANES, LANES), 0) // HEAD
    pick_cols = lax.broadcasted_iota(jnp.int32, (LANES, LANES), 1)
    g_meeting = jnp.zeros((width, width), f32)
    by_row = []
    per_head = jnp.zeros((3 * width + 8, LANES), f32)
    g_entry = jnp.zeros((width, N), f32)
    g_readout = jnp.zeros((width, N), f32)
    for p in range(local // LANES):
        at = slice(p * LANES, (p + 1) * LANES)
        signal = active[:, at]
        g_y = g_result[:, at].astype(f32)
        steps_p = spread_pair(low, steps, p)
        entered = signal * steps_p
        g_mixing = dot_nt(stacked(low, entered), g_result[:, at])
        mixing, along, parts = [], [], []
        for k, h in enumerate((2 * p, 2 * p + 1)):
            along.append(jnp.broadcast_to(running[:, h : h + 1], (width, width)))
            span = jnp.minimum(across[h : h + 1, :] - along[-1], 0.0)
            kernel = jnp.exp(span)
            mixing.append((kernel * meeting).astype(bf16))
            part = g_mixing[k * width : (k + 1) * width, :] * kernel
            g_meeting = g_meeting + part
            parts.append((part * meeting).astype(bf16))
            by_row.append(jnp.sum(parts[-1].astype(f32), axis=0, keepdims=True))
        across_sum = dot(jnp.concatenate(parts, axis=0), ones)
        for k, h in enumerate((2 * p, 2 * p + 1)):
            by_col = jnp.where(lane == h, across_sum[k * width : (k + 1) * width], by_col)
        along = jnp.where(low, along[0], along[1])
        grown_p = jnp.exp(along)
        left_p = jnp.exp(along[width - 1 : width, :] - along)
        back = left_p * returned[:, at]
        through = dot(jnp.concatenate(mixing, axis=1), stacked(low, g_y)) + back
        skip = by_channel[6:7, at]
        ahead[0:width, at] = steps_p * through + skip * g_y
        sum_channel[5:6, at] += jnp.sum(g_y * signal, axis=0, keepdims=True)
        g_grown = grown_p * g_y
        g_grown_b = g_grown.astype(bf16)
        before_p = before[:, at]
        after_p = adjoint[:, at]
        held = jnp.sum(after_p * before_p.astype(f32), axis=0, keepdims=True)
        pieces = jnp.concatenate(
            [
                signal * through,
                entered * back,
                g_grown * carried[:, at],
                jnp.broadcast_to(held, (8, LANES)),
            ],
            axis=0,
        )
        pick = jnp.where(pick_rows + 2 * p == pick_cols, 1.0, 0.0)
        per_head = per_head + dot(pieces.astype(bf16), pick.astype(bf16))
        g_readout = g_readout + dot_nt(g_grown_b, before_p)
        g_entry = g_entry + dot_nt((left_p * entered).astype(bf16), after[:, at])
        adjoint[:, at] = grown_p[width - 1 : width, :] * after_p + dot(readout_t, g_grown_b)
    g_meeting = jnp.where(rows <= cols, g_meeting, 0.0)
    g_readout = g_readout + dot(g_meeting.T.astype(bf16), entry_b)
    g_entry = g_entry + dot(g_meeting.astype(bf16), readout_b)
    heads = len(by_row)
    by_row = jnp.concatenate(by_row + [jnp.zeros((LANES - heads, width), f32)], axis=0).T
    direct = per_head[0:width]
    entering = per_head[width : 2 * width]
    rising = by_row + per_head[2 * width : 3 * width] - by_col
    change = entering - rising
    g_falls = (
        running_sum(change)
        - change
        + jnp.sum(rising, axis=0, keepdims=True)
        + jnp.exp(running[width - 1 : width, :]) * per_head[3 * width : 3 * width + 1]
    )
    g_steps = rate * g_falls + direct
    g_raw = g_steps * sigmoid(shifted)
    sum_head[0:1, :] += jnp.sum(g_raw, axis=0, keepdims=True)
    sum_head[1:2, :] += jnp.sum(falls * g_falls, axis=0, keepdims=True)
    g_projected[:, local + channels :] = g_raw.astype(bf16)
    ahead[0:width, local : local + N] = g_entry
    ahead[0:width, local + N :] = g_readout
    g_filtered = ahead[0:width, :] * slope
    ahead[0:width, :] = g_filtered
    g_in = jnp.zeros((width, channels), f32)
    for tap in range(taps):
        back_at = taps - 1 - tap
        g_in = g_in + by_channel[tap : tap + 1, :] * ahead[back_at : back_at + width, :]
        at = 9 - taps + tap
        sum_channel[tap : tap + 1, :] += jnp.sum(
            g_filtered * window[at : at + width, :], axis=0, keepdims=True
        )
    sum_channel[4:5, :] += jnp.sum(g_filtered, axis=0, keepdims=True)
    g_projected[:, local : local + channels] = g_in.astype(bf16)


def reversed_bits(chip, count):
    bits = count.bit_length() - 1
    return sum(((chip >> k) & 1) << (bits - 1 - k) for k in range(bits))


def slot_of(place, rank, pieces):
    count = pieces // 2
    half = count // 2
    core = (place ^ rank) & 1
    chip = (place ^ rank) >> 1
    at = jnp.where(core == 0, chip, reversed_bits(chip, count))
    return jnp.where(at < half, count, -half) + core * half + at


def chip_order(turn, count):
    return [j if turn == 0 else reversed_bits(j, count) for j in range(count)]


def slot_order(count):
    half = count // 2
    orders = [chip_order(turn, count) for turn in range(2)]
    return [
        (turn, orders[turn][upper * half + low])
        for upper in (1, 0)
        for turn in range(2)
        for low in range(half)
    ]


def scan_forward(rank, projected, by_channel, by_head, local, width):
    length, columns = projected.shape
    count = length // width
    channels = local + 2 * N

    def here(i, rank):
        return (slot_of(i, rank[0], count), 0)

    def fixed(i, rank):
        return (0, 0)

    return pl.pallas_call(
        forward_kernel,
        grid_spec=pltpu.PrefetchScalarGridSpec(
            num_scalar_prefetch=1,
            grid=(count,),
            in_specs=[
                pl.BlockSpec((width, columns), here),
                pl.BlockSpec((8, channels), fixed),
                pl.BlockSpec((8, LANES), fixed),
            ],
            out_specs=[
                pl.BlockSpec((width, local), here),
                pl.BlockSpec((width, local), here),
                pl.BlockSpec((width, 1), here),
                pl.BlockSpec((1, N, local), lambda i, rank: (i, 0, 0)),
            ],
            scratch_shapes=[
                pltpu.VMEM((N, local), f32),
                pltpu.VMEM((width + 8, channels), f32),
            ],
        ),
        out_shape=[
            jax.ShapeDtypeStruct((length, local), f32),
            jax.ShapeDtypeStruct((length, local), bf16),
            jax.ShapeDtypeStruct((length, 1), f32),
            jax.ShapeDtypeStruct((count, N, local), bf16),
        ],
        compiler_params=pltpu.CompilerParams(vmem_limit_bytes=VMEM),
        cost_estimate=pl.CostEstimate(flops=1_000_000, bytes_accessed=1_000_000, transcendentals=0),
        name="scan_forward",
    )(rank, projected, by_channel, by_head)


def scan_backward(rank, projected, g_result, g_gate, states, by_channel, by_head, width):
    length, columns = projected.shape
    local = g_result.shape[1]
    count = length // width
    channels = local + 2 * N

    def here(i, rank):
        return (slot_of(count - 1 - i, rank[0], count), 0)

    def tail(i, rank):
        earlier = jnp.maximum(count - 2 - i, 0)
        return (slot_of(earlier, rank[0], count) * (width // 8) + (width // 8 - 1), 0)

    def fixed(i, rank):
        return (0, 0)

    return pl.pallas_call(
        backward_kernel,
        grid_spec=pltpu.PrefetchScalarGridSpec(
            num_scalar_prefetch=1,
            grid=(count,),
            in_specs=[
                pl.BlockSpec((width, columns), here),
                pl.BlockSpec((8, columns), tail),
                pl.BlockSpec((width, local), here),
                pl.BlockSpec((width, local), here),
                pl.BlockSpec((1, N, local), lambda i, rank: (count - 1 - i, 0, 0)),
                pl.BlockSpec((8, channels), fixed),
                pl.BlockSpec((8, LANES), fixed),
            ],
            out_specs=[
                pl.BlockSpec((width, columns), here),
                pl.BlockSpec((8, channels), fixed),
                pl.BlockSpec((8, LANES), fixed),
            ],
            scratch_shapes=[
                pltpu.VMEM((N, local), f32),
                pltpu.VMEM((width + 8, channels), f32),
                pltpu.VMEM((width + 8, channels), f32),
            ],
        ),
        out_shape=[
            jax.ShapeDtypeStruct((length, columns), bf16),
            jax.ShapeDtypeStruct((8, channels), f32),
            jax.ShapeDtypeStruct((8, LANES), f32),
        ],
        compiler_params=pltpu.CompilerParams(vmem_limit_bytes=VMEM),
        cost_estimate=pl.CostEstimate(flops=1_000_000, bytes_accessed=1_000_000, transcendentals=0),
        name="scan_backward",
    )(rank, projected, projected, g_result, g_gate, states, by_channel, by_head)


BELOW = 16


def pack_kernel(
    place,
    in_weight,
    step_weight,
    filter_weight,
    filter_bias,
    inner_gain,
    norm_gain,
    per_head,
    *refs,
):
    parts, spread = refs[:-1], refs[-1]
    chips = len(parts)
    rows, columns = in_weight.shape[0], parts[0].shape[1]
    heads = step_weight.shape[1]
    local = (columns - 2 * N - LANES) // 2
    inner = local * chips
    channels = local + 2 * N
    each = heads // chips
    chip, core = place[0], place[1]
    taps, mine = filter_weight.shape
    at_row = lax.broadcasted_iota(jnp.int32, (heads, LANES), 0)
    at_lane = lax.broadcasted_iota(jnp.int32, (heads, LANES), 1)

    def laid(a, width, at):
        a = jnp.pad(a.astype(f32), ((0, 0), (0, width - a.shape[1])))
        return pltpu.roll(a, at, 1)

    filters = jnp.concatenate(
        [
            filter_weight[...].astype(f32),
            filter_bias[...].astype(f32),
            jnp.zeros((8 - taps - 1, mine), f32),
        ],
        axis=0,
    )
    spread[...] = laid(filters, spread.shape[1], (2 * chip + core) * mine)
    gain = laid(norm_gain[...], -(-chips * rows // LANES) * LANES, chip * rows)
    inner_row = laid(inner_gain[...], local, core * inner_gain.shape[1])
    head_rows = laid(per_head[...], LANES, core * (each // 2))
    for j in range(chips):
        c = chip ^ j
        out = parts[j]
        at = pl.ds(0, rows)
        from_gate = pl.ds(pl.multiple_of(c * local, LANES), local)
        out[at, 0:local] = in_weight[:, from_gate]
        out[at, local : 2 * local] = in_weight[
            :, pl.ds(pl.multiple_of(inner + c * local, LANES), local)
        ]
        out[at, 2 * local : 2 * local + 2 * N] = in_weight[:, 2 * inner :]
        pick = jnp.logical_and(at_row == c * each + at_lane, at_lane < each)
        pick = jnp.where(pick, 1.0, 0.0).astype(bf16)
        out[at, 2 * local + 2 * N :] = dot(step_weight[...], pick).astype(bf16)
        top = jnp.concatenate([spread[:, from_gate], spread[:, inner:]], axis=1)
        if j == 0:
            row = lax.broadcasted_iota(jnp.int32, (8, channels), 0)
            wide = jnp.pad(inner_row, ((0, 0), (0, 2 * N)))
            top = jnp.where(row == 5, wide, top)
        low = [jnp.zeros((8, LANES), f32) if j else head_rows, jnp.broadcast_to(gain, (8, gain.shape[1]))]
        low = jnp.concatenate(low, axis=1)
        low = jnp.pad(low, ((0, 0), (0, columns - low.shape[1])))
        top = jnp.pad(top, ((0, 0), (0, columns - channels)))
        out[rows:, :] = jnp.concatenate([top, low], axis=0).astype(bf16)


def pack_columns(place, arrays, per_head, chips, columns, inner):
    rows = arrays[0].shape[0] + BELOW
    vmem = pl.BlockSpec(memory_space=pltpu.VMEM)
    return pl.pallas_call(
        pack_kernel,
        in_specs=[pl.BlockSpec(memory_space=pltpu.SMEM)] + [vmem] * (len(arrays) + 1),
        out_specs=[vmem] * chips,
        out_shape=[jax.ShapeDtypeStruct((rows, columns), bf16)] * chips,
        scratch_shapes=[pltpu.VMEM((8, inner + 2 * N), f32)],
        compiler_params=pltpu.CompilerParams(vmem_limit_bytes=VMEM),
        cost_estimate=pl.CostEstimate(flops=1_000_000, bytes_accessed=1_000_000, transcendentals=0),
        name="pack_columns",
    )(place, *arrays, per_head)


def parameter_kernel(side, *refs):
    parts, (by_channel, by_head, gain) = refs[:-3], refs[-3:]
    channels = by_channel.shape[1]
    half = len(parts) // 2
    sums = [
        sum((part[...].astype(f32) for part in parts[k * half + 1 : (k + 1) * half]), parts[k * half][...].astype(f32))
        for k in range(2)
    ]
    whole = sums[0] + sums[1]
    heads = whole[8:16, 0:LANES]
    head = lax.broadcasted_iota(jnp.int32, (LANES, channels), 0)
    lane = lax.broadcasted_iota(jnp.int32, (LANES, channels), 1)
    expand = jnp.where(head == lane // HEAD, 1.0, 0.0).astype(bf16)
    skip = dot(heads[2:3].astype(bf16), expand)
    row = lax.broadcasted_iota(jnp.int32, (8, channels), 0)
    by_channel[...] = jnp.where(row == 6, skip, whole[0:8, 0:channels])
    row = lax.broadcasted_iota(jnp.int32, (8, LANES), 0)
    by_head[...] = jnp.where(
        row == 0, heads, jnp.where(row == 1, -jnp.exp(heads), 0.0)
    )
    gain[:, 0:side] = sums[0][8:9, LANES : LANES + side]
    gain[:, side:] = sums[1][8:9, LANES : LANES + side]


def parameters(parts, channels, width):
    total, columns = parts[0].shape
    at = total // BELOW - 1

    def whole(shape):
        return pl.BlockSpec(shape, lambda i: (0, 0))

    shapes = [(8, channels), (8, LANES), (1, width)]
    return pl.pallas_call(
        lambda *refs: parameter_kernel(width // 2, *refs),
        grid=(1,),
        in_specs=[pl.BlockSpec((BELOW, columns), lambda i: (at, 0))] * len(parts),
        out_specs=[whole(shape) for shape in shapes],
        out_shape=[jax.ShapeDtypeStruct(shape, f32) for shape in shapes],
        compiler_params=pltpu.CompilerParams(vmem_limit_bytes=VMEM),
        cost_estimate=pl.CostEstimate(flops=1_000_000, bytes_accessed=1_000_000, transcendentals=0),
        name="parameters",
    )(*parts)


def assemble_kernel(place, *refs):
    parts, out = refs[:-1], refs[-1]
    chips = len(parts) // 2
    rows = parts[0].shape[0] - BELOW
    for k in range(2):
        for j in range(chips):
            at = pl.multiple_of((k * chips + (place[0] ^ j)) * rows, BELOW)
            out[pl.ds(at, rows), :] = parts[k * chips + j][0:rows, :]


def assembled(place, parts):
    vmem = pl.BlockSpec(memory_space=pltpu.VMEM)
    rows, columns = parts[0].shape
    return pl.pallas_call(
        assemble_kernel,
        in_specs=[pl.BlockSpec(memory_space=pltpu.SMEM)] + [vmem] * len(parts),
        out_specs=vmem,
        out_shape=jax.ShapeDtypeStruct(((rows - BELOW) * len(parts), columns), bf16),
        compiler_params=pltpu.CompilerParams(vmem_limit_bytes=VMEM),
        cost_estimate=pl.CostEstimate(flops=1_000_000, bytes_accessed=1_000_000, transcendentals=0),
        name="assembled",
    )(place, *parts)


def split_kernel(ranks, core, tokens, mine, sent):
    batch, piece, width = tokens.shape
    half = batch // 2
    rows = width // ranks
    first = core[0] == 0
    for b in range(batch):
        parts = [
            jnp.concatenate(
                [
                    tokens[b, :, c * rows : (c + 1) * rows].astype(f32)
                    for c in range(k, ranks, 2)
                ],
                axis=1,
            )
            for k in range(2)
        ]
        own = jnp.where(first, parts[0], parts[1])
        other = jnp.where(first, parts[1], parts[0])
        here = first if b < half else jnp.logical_not(first)

        @pl.when(here)
        def _():
            mine[b % half] = jnp.concatenate([own, other], axis=1).astype(bf16)

        @pl.when(jnp.logical_not(here))
        def _():
            sent[b % half] = jnp.concatenate([other, own], axis=1).astype(bf16)


def split_tokens(core, tokens, ranks):
    batch, piece, width = tokens.shape
    vmem = pl.BlockSpec(memory_space=pltpu.VMEM)
    shape = jax.ShapeDtypeStruct((batch // 2, piece, width), bf16)
    return pl.pallas_call(
        lambda *refs: split_kernel(ranks, *refs),
        in_specs=[pl.BlockSpec(memory_space=pltpu.SMEM), vmem],
        out_specs=[vmem, vmem],
        out_shape=[shape, shape],
        compiler_params=pltpu.CompilerParams(vmem_limit_bytes=VMEM),
        cost_estimate=pl.CostEstimate(flops=1_000_000, bytes_accessed=1_000_000, transcendentals=0),
        name="split_tokens",
    )(core, tokens)


def distinct(pieces):
    arrays, where = [], []
    for array, index in pieces:
        found = [k for k, a in enumerate(arrays) if a is array]
        if not found:
            arrays.append(array)
            found = [len(arrays) - 1]
        where.append((found[0], index))
    return arrays, where


def rows_call(kernel, pieces, extra, name):
    arrays, where = distinct(pieces)
    vmem = pl.BlockSpec(memory_space=pltpu.VMEM)
    rows, width = arrays[0].shape[1:]
    return pl.pallas_call(
        lambda *refs: kernel(where, *refs),
        in_specs=[vmem] * (len(arrays) + len(extra)),
        out_specs=vmem,
        out_shape=jax.ShapeDtypeStruct((rows * len(where), width), bf16),
        compiler_params=pltpu.CompilerParams(vmem_limit_bytes=VMEM),
        cost_estimate=pl.CostEstimate(flops=1_000_000, bytes_accessed=1_000_000, transcendentals=0),
        name=name,
    )(*extra, *arrays)


def project_kernel(where, gain, columns, *refs):
    pieces, (out, projected) = refs[:-2], refs[-2:]
    rows = pieces[0].shape[1]

    @pl.when(pl.program_id(0) == 0)
    def _():
        for k, (a, index) in enumerate(where):
            values = pieces[a][index].astype(f32)
            scale = lax.rsqrt(jnp.mean(values * values, axis=1, keepdims=True) + EPSILON)
            out[k * rows : (k + 1) * rows, :] = (values * scale * gain[...]).astype(bf16)

    tile = 256
    for k in range(out.shape[0] // tile):
        at = slice(k * tile, (k + 1) * tile)
        projected[at, :] = dot(out[at, :], columns[...])


def project(pieces, gain, columns):
    arrays, where = distinct(pieces)
    rows, width = arrays[0].shape[1:]
    length, wide = rows * len(where), columns.shape[1]
    tile = 384 if wide % 384 == 0 else LANES

    def whole(shape):
        return pl.BlockSpec(shape, lambda i: (0,) * len(shape))

    return pl.pallas_call(
        lambda *refs: project_kernel(where, *refs),
        grid=(wide // tile,),
        in_specs=[whole(gain.shape), pl.BlockSpec((width, tile), lambda i: (0, i))]
        + [whole(a.shape) for a in arrays],
        out_specs=[whole((length, width)), pl.BlockSpec((length, tile), lambda i: (0, i))],
        out_shape=[
            jax.ShapeDtypeStruct((length, width), bf16),
            jax.ShapeDtypeStruct((length, wide), f32),
        ],
        compiler_params=pltpu.CompilerParams(vmem_limit_bytes=VMEM),
        cost_estimate=pl.CostEstimate(flops=1_000_000, bytes_accessed=1_000_000, transcendentals=0),
        name="project",
    )(gain, columns, *arrays)


def joined_kernel(where, *refs):
    pieces, out = refs[:-1], refs[-1]
    rows = pieces[0].shape[1]
    for k, (a, index) in enumerate(where):
        out[k * rows : (k + 1) * rows, :] = pieces[a][index]


def joined_rows(pieces):
    return rows_call(joined_kernel, pieces, [], "joined_rows")


def gate_kernel(result, projected, g_mixed, norms, by_channel, g_result, g_gate, mixed):
    local = result.shape[1]
    gain = by_channel[5:6, 0:local]
    r = norms[:, 0:1]
    y = result[...]
    gate = projected[...]
    gate_s = sigmoid(gate)
    silu = gate * gate_s
    gated = y * silu
    mixed[...] = (gated * r * gain).astype(bf16)
    g_gated = r * gain * g_mixed[...] - gated * norms[:, 1:2]
    g_result[...] = (g_gated * silu).astype(bf16)
    g_gate[...] = (g_gated * y * gate_s * (1.0 + gate * (1.0 - gate_s))).astype(bf16)


def gate_gradients(result, projected, g_mixed, norms, by_channel):
    length, local = result.shape
    width = 256

    def here(i):
        return (i, 0)

    block = pl.BlockSpec((width, local), here)
    return pl.pallas_call(
        gate_kernel,
        grid=(length // width,),
        in_specs=[
            block,
            block,
            block,
            pl.BlockSpec((width, 2), here),
            pl.BlockSpec(by_channel.shape, lambda i: (0, 0)),
        ],
        out_specs=[block] * 3,
        out_shape=[jax.ShapeDtypeStruct((length, local), bf16)] * 3,
        compiler_params=pltpu.CompilerParams(vmem_limit_bytes=VMEM),
        cost_estimate=pl.CostEstimate(flops=1_000_000, bytes_accessed=1_000_000, transcendentals=0),
        name="gate_gradients",
    )(result, projected, g_mixed, norms, by_channel)


def output_kernel(core, tokens, kept, got, output):
    batch = tokens.shape[0]
    half = batch // 2
    for b in range(batch):
        mine = core[0] == b // half
        total = jnp.where(mine, kept[b % half], got[b % half].astype(f32))
        output[b] = (tokens[b].astype(f32) + total).astype(bf16)


def token_kernel(ranks, core, tokens, cotangent, gain, kept, got, gradient):
    batch, _, width = tokens.shape
    half, side, rows = batch // 2, width // 2, width // ranks
    gains = (gain[:, :side], gain[:, side:])
    first = core[0] == 0
    gains = (jnp.where(first, gains[0], gains[1]), jnp.where(first, gains[1], gains[0]))
    for b in range(batch):
        owner = b // half
        g = jnp.where(core[0] == owner, kept[b % half], got[b % half].astype(f32))
        parts = (g[:, :side], g[:, side:]) if owner == 0 else (g[:, side:], g[:, :side])
        parts = (parts[0] * gains[0], parts[1] * gains[1])
        weighted = jnp.concatenate(
            [part[:, c * rows : (c + 1) * rows] for c in range(ranks // 2) for part in parts],
            axis=1,
        )
        values = tokens[b].astype(f32)
        scale = lax.rsqrt(jnp.mean(values * values, axis=1, keepdims=True) + EPSILON)
        inner = jnp.mean(values * weighted, axis=1, keepdims=True)
        gradient[b] = (
            cotangent[b].astype(f32) + scale * weighted - values * (scale * scale * scale * inner)
        )


def share_kernel(chips, place, summed, *parts):
    share, columns = parts[0].shape
    width = summed.shape[1]
    for j in range(chips):
        c = place[0] ^ j
        for k in range(columns // width):
            at = pl.multiple_of((k * chips + c) * share, share)
            parts[j][:, k * width : (k + 1) * width] = summed[pl.ds(at, share), :]


def shares_by_chip(place, summed, chips, share, columns):
    vmem = pl.BlockSpec(memory_space=pltpu.VMEM)
    return pl.pallas_call(
        lambda *refs: share_kernel(chips, *refs),
        in_specs=[pl.BlockSpec(memory_space=pltpu.SMEM), vmem],
        out_specs=[vmem] * chips,
        out_shape=[jax.ShapeDtypeStruct((share, columns), bf16)] * chips,
        compiler_params=pltpu.CompilerParams(vmem_limit_bytes=VMEM),
        cost_estimate=pl.CostEstimate(flops=1_000_000, bytes_accessed=1_000_000, transcendentals=0),
        name="shares_by_chip",
    )(place, summed)


def early_kernel(across, place, summed, *refs):
    parts, out = refs[:-1], refs[-1]
    share, local = parts[0].shape
    chips = len(parts)
    inner = chips * local
    for j, part in enumerate(parts):
        out[:, pl.ds(pl.multiple_of((place[0] ^ j) * local, LANES), local)] = part[...]
    rounds = (summed.shape[0] // share - chips) // across
    for k in range(across):
        for r in range(rounds):
            start = chips * share + (k * rounds + r) * share
            to = inner + (r * across + k) * local
            out[:, to : to + local] = summed[start : start + share, :]


def late_kernel(heads, place, *refs):
    parts, out = refs[:-1], refs[-1]
    chips = len(parts)
    each = heads // chips
    columns = parts[0].shape[1]
    local = columns - 2 * N - LANES
    inner = chips * local
    row = lax.broadcasted_iota(jnp.int32, (LANES, heads), 0)
    lane = lax.broadcasted_iota(jnp.int32, (LANES, heads), 1)
    steps = jnp.zeros((out.shape[0], heads), f32)
    shared = jnp.zeros((out.shape[0], 2 * N), f32)
    for j, part in enumerate(parts):
        c = place[0] ^ j
        out[:, pl.ds(pl.multiple_of(c * local, LANES), local)] = part[:, 0:local]
        shared = shared + part[:, local : local + 2 * N].astype(f32)
        pick = jnp.logical_and(lane == c * each + row, row < each)
        steps = steps + dot(part[:, local + 2 * N :], jnp.where(pick, 1.0, 0.0).astype(bf16))
    out[:, inner : inner + 2 * N] = shared.astype(bf16)
    out[:, inner + 2 * N :] = steps.astype(bf16)


def joined_shares(kernel, place, arrays, shape, name):
    vmem = pl.BlockSpec(memory_space=pltpu.VMEM)
    return pl.pallas_call(
        kernel,
        in_specs=[pl.BlockSpec(memory_space=pltpu.SMEM)] + [vmem] * len(arrays),
        out_specs=vmem,
        out_shape=jax.ShapeDtypeStruct(shape, bf16),
        compiler_params=pltpu.CompilerParams(vmem_limit_bytes=VMEM),
        cost_estimate=pl.CostEstimate(flops=1_000_000, bytes_accessed=1_000_000, transcendentals=0),
        name=name,
    )(place, *arrays)


def weights_kernel(early, rest, in_weight, step_weight, total_in, total_step, by_gain):
    inner = in_weight.shape[1] - 2 * N - early_columns(in_weight)
    heads = step_weight.shape[1]
    first = early[:, 0:inner].astype(f32)
    last = rest[:, 0 : inner + 2 * N].astype(f32)
    step = rest[:, inner + 2 * N :].astype(f32)
    total_in[:, 0:inner] = first
    total_in[:, inner:] = last
    total_step[...] = step
    by_gain[...] = (
        jnp.sum(in_weight[:, 0:inner].astype(f32) * first, axis=1, keepdims=True)
        + jnp.sum(in_weight[:, inner:].astype(f32) * last, axis=1, keepdims=True)
        + jnp.sum(step_weight[...].astype(f32) * step, axis=1, keepdims=True)
    )


def early_columns(in_weight):
    return (in_weight.shape[1] - 2 * N) // 2


def weight_totals(early, rest, in_weight, step_weight):
    rows = in_weight.shape[0]
    block = rows // 4 if rows % 64 == 0 else rows

    def here(i):
        return (i, 0)

    arrays = [early, rest, in_weight, step_weight]
    widths = [in_weight.shape[1], step_weight.shape[1], 1]
    return pl.pallas_call(
        weights_kernel,
        grid=(rows // block,),
        in_specs=[pl.BlockSpec((block, a.shape[1]), here) for a in arrays],
        out_specs=[pl.BlockSpec((block, width), here) for width in widths],
        out_shape=[jax.ShapeDtypeStruct((rows, width), f32) for width in widths],
        compiler_params=pltpu.CompilerParams(vmem_limit_bytes=VMEM),
        cost_estimate=pl.CostEstimate(flops=1_000_000, bytes_accessed=1_000_000, transcendentals=0),
        name="weight_totals",
    )(*arrays)


def whole_call(kernel, scalar, arrays, shape, dtype, name):
    vmem = pl.BlockSpec(memory_space=pltpu.VMEM)
    return pl.pallas_call(
        kernel,
        in_specs=[pl.BlockSpec(memory_space=pltpu.SMEM)] + [vmem] * len(arrays),
        out_specs=vmem,
        out_shape=jax.ShapeDtypeStruct(shape, dtype),
        compiler_params=pltpu.CompilerParams(vmem_limit_bytes=VMEM),
        cost_estimate=pl.CostEstimate(flops=1_000_000, bytes_accessed=1_000_000, transcendentals=0),
        name=name,
    )(scalar, *arrays)


def across_chips(x, bit):
    return lax.ppermute(x, "chip", [(i, i ^ bit) for i in range(lax.axis_size("chip"))])


def sibling(x):
    return lax.ppermute(x, "core", [(0, 1), (1, 0)])


def chip_bits(turn):
    chips = lax.axis_size("chip")
    bits = [1 << k for k in range(chips.bit_length() - 1)]
    return bits if turn == 0 else bits[::-1]


def after(x, *deps):
    return lax.optimization_barrier((x, deps))[0]


class Gather:
    def __init__(self, block):
        self.own = {bit: across_chips(block, bit) for bit in chip_bits(0)}
        self.have = []
        for turn in range(2):
            have = {0: (block, turn)}
            for bit in chip_bits(turn)[:1]:
                have[bit] = (self.own[bit], turn)
            self.have.append(have)

    def received(self):
        return list(self.own.values())

    def relay(self, *deps):
        relayed = []
        for turn, have in enumerate(self.have):
            for bit in chip_bits(turn)[1:]:
                new = {bit: (self.own[bit], turn)}
                for j, (array, index) in sorted(have.items()):
                    if j:
                        part = array[index : index + 1]
                        part = after(part, *deps) if deps else part
                        relayed.append(part)
                        new[j ^ bit] = (across_chips(part, bit), 0)
                have.update(new)
        return relayed

    def slots(self):
        return [self.have[turn][j] for turn, j in slot_order(len(self.have[0]))]


class Scatter:
    def __init__(self, rows, chips, *deps, keep_rows=None):
        self.rows = keep_rows or rows
        self.bits = [chip_bits(turn)[::-1] for turn in range(2)]
        gives = tuple(part.astype(bf16) for part in rows(True))
        self.gives = after(gives, *deps) if deps else gives
        self.kept = None
        self.sent = [across_chips(x, bits[0]) for x, bits in zip(self.gives, self.bits)]

    def step(self, *deps):
        kept = self.rows(False) if self.kept is None else self.kept
        sent = after(tuple(self.sent), *deps) if deps else self.sent
        self.kept, self.sent = [], []
        for turn, bits in enumerate(self.bits):
            bits.pop(0)
            total = kept[turn].astype(f32) + sent[turn].astype(f32)
            if bits:
                half = total.shape[0] // 2
                self.kept.append(total[:half])
                self.sent.append(across_chips(total[half:].astype(bf16), bits[0]))
            else:
                self.kept.append(total)

    def done(self, *deps):
        while self.bits[0]:
            self.step(*deps)
        return [part[0] for part in self.kept]


def chip_total(x):
    order = slot_order(x.shape[-2] // 2)
    for bit in chip_bits(0):
        moved = [order.index((turn, j ^ bit)) for turn, j in order]
        pick = jnp.asarray([[float(m == k) for k in range(len(order))] for m in moved], f32)
        x = x + jnp.einsum("st,atp->asp", pick, across_chips(x, bit), precision=precise)
    return x


def across_groups(x, step):
    return lax.ppermute(x, "dp", [(i, i ^ step) for i in range(lax.axis_size("dp"))])


def by_group(x):
    blocks, rows, width = x.shape
    count = lax.axis_size("dp")
    return x.reshape(blocks, count, rows // count, width).transpose(1, 0, 2, 3)


def group_scatter(x):
    return lax.psum_scatter(x, "dp", scatter_dimension=0, tiled=False)


def group_gather(x):
    return lax.all_gather(x, "dp", axis=0, tiled=True)


def body(
    tokens,
    norm_gain,
    in_weight,
    step_weight,
    filter_weight,
    filter_bias,
    step_bias,
    log_rate,
    skip_scale,
    inner_gain,
    out_weight,
    cotangent,
):
    chips = lax.axis_size("chip")
    chip, core = lax.axis_index("chip"), lax.axis_index("core")
    rank = chip * 2 + core
    batch, piece, width = tokens.shape
    half = batch // 2
    ranks = chips * 2
    heads = log_rate.shape[0] * ranks
    inner = inner_gain.shape[0] * ranks
    local_heads, local = heads // chips, inner // chips
    rows = in_weight.shape[0]
    side = width // 2
    taps = filter_weight.shape[0]
    channels = local + 2 * N
    first = core == 0

    def own_first(a, b):
        return (jnp.where(first, a, b), jnp.where(first, b, a))

    columns_in = 2 * local + 2 * N + LANES
    place = jnp.stack([chip, core]).astype(jnp.int32)
    per_head = jnp.stack([step_bias, log_rate, skip_scale])
    per_head = jnp.pad(per_head, ((0, 5), (0, 0)))
    packed_weight = pack_columns(
        place,
        [
            in_weight,
            step_weight,
            filter_weight,
            filter_bias[None],
            inner_gain[None],
            norm_gain[None],
        ],
        per_head,
        chips,
        columns_in,
        inner,
    )

    def of_core(a, which):
        return lax.dynamic_slice_in_dim(a, which * half, half, 0)

    core_ref = core.astype(jnp.int32).reshape(1)
    mine, sent = split_tokens(after(core_ref, *packed_weight), tokens, ranks)
    got = sibling(sent)
    token_blocks = [jnp.stack([mine[b], got[b]]) for b in range(half)]
    mine_cot, got_cot = of_core(cotangent, core), sibling(of_core(cotangent, 1 - core))
    cot_blocks = [jnp.stack([mine_cot[b], got_cot[b]]) for b in range(half)]

    parts = [across_chips(part, j) if j else part for j, part in enumerate(packed_weight)]
    parts = parts + [sibling(part) for part in parts]
    by_channel, by_head, gain = parameters(parts, channels, width)
    columns = assembled(place, parts)
    out_low, out_high = own_first(out_weight, sibling(out_weight))
    out_rows = jnp.concatenate([out_low, out_high], axis=0)

    def tn(a, b):
        return lax.dot_general(a, b, (((0,), (0,)), ((), ())), preferred_element_type=f32)

    rank_ref = rank.astype(jnp.int32).reshape(1)
    spans = range(half)
    queue = [Gather(token_blocks[0])]
    for block in token_blocks[1:] + cot_blocks:
        queue.append((block, None))
    moved = 0

    def advance(*deps):
        nonlocal moved
        if moved >= len(queue):
            return []
        now = queue[moved]
        before = [part for part, _ in queue[moved - 1].slots()] if moved else []
        relayed = now.relay(*deps, *before)
        moved += 1
        if moved < len(queue):
            waits = now.received() if moved > 1 else [part for part, _ in now.slots()]
            block = after(queue[moved][0], *waits, *deps)
            queue[moved] = Gather(block)
            relayed = relayed + [block]
        return relayed

    def slot_rows(a, run):
        count = a.shape[0] // 2

        def rows(upper):
            part = run(a[:count] if upper else a[count:])
            return part.reshape(2, chips // 2, piece, width)

        return rows

    advance()
    normed, projected, fronts = [], [], []
    for b in spans:
        ready = after(gain, fronts[b - 1][2]) if b else gain
        normed_b, projected_b = project(queue[b].slots(), ready, columns)
        normed.append(normed_b)
        projected.append(projected_b)
        issued = advance(*([projected[0]] if b == 0 else []))
        fronts.append(
            scan_forward(
                rank_ref, projected[b], by_channel, after(by_head, *issued), local, piece
            )
        )
        if b + 1 < half:
            advance(fronts[b][2])
    while moved < len(queue):
        advance(fronts[-1][2])
    cots = queue[half:]

    all_cot, g_mixed, stats, local_stats = [], [], [], []
    for b in spans:
        result, scaled, squares, states = fronts[b]
        all_cot.append(joined_rows(cots[b].slots()))
        g_mixed.append(dot_nt(all_cot[b], out_rows))
        both = jnp.stack([squares[:, 0], jnp.sum(scaled.astype(f32) * g_mixed[b], axis=1)])
        local_stats.append(both)
        stats.append(chip_total(both.reshape(2, ranks, piece)).reshape(both.shape) / inner)
    g_results, g_gates, mixed, outs = [], [], [], []
    for b in spans:
        r = lax.rsqrt(stats[b][0] + EPSILON)
        norms = jnp.stack([r, r * r * r * stats[b][1]], axis=1)
        if b + 1 < half:
            norms = after(norms, local_stats[b + 1])
        g_result, g_gate, mixed_b = gate_gradients(
            fronts[b][0], projected[b], g_mixed[b], norms, by_channel
        )
        g_results.append(g_result)
        g_gates.append(g_gate)
        mixed.append(mixed_b)
        outs.append(Scatter(slot_rows(mixed_b, lambda x: dot(x, out_rows)), chips, stats[-1]))

    def row_sums(parts):
        far = [tn(normed[b][:, side:], parts[b]) for b in range(len(parts))]
        near = [tn(normed[b][:, :side], parts[b]) for b in range(len(parts))]
        return far, near

    def core_sum(far, near, *deps):
        sent = after(sum(far).astype(bf16), *deps)
        total = (sum(near) + sibling(sent).astype(f32)).astype(bf16)
        return total.reshape(chips, rows, -1)

    def by_chip(near):
        found = []
        for j in range(chips):
            part = lax.dynamic_index_in_dim(near, chip ^ j, 0, keepdims=True)
            found.append(across_chips(part, j) if j else part)
        return found

    def exchanged(parts):
        return [across_chips(part, j) if j else part for j, part in enumerate(parts)]

    def in_place(parts, size, total):
        whole = jnp.zeros(parts[0].shape[:2] + (total,), bf16)
        for j, part in enumerate(parts):
            whole = lax.dynamic_update_slice_in_dim(whole, part[:, :, :size], (chip ^ j) * size, 2)
        return whole

    gate_near = core_sum(*row_sums(g_gates))
    out_gradient = sum(tn(mixed[b], all_cot[b]) for b in spans)
    out_near, out_far = own_first(out_gradient[: local // 2], out_gradient[local // 2 :])
    out_near = (out_near + sibling(out_far.astype(bf16)).astype(f32)).astype(bf16)
    groups = lax.axis_size("dp")
    share = rows // groups
    out_near = out_near.reshape(groups, -1, width)
    out_near = jnp.concatenate(
        [out_near[:, :, k : k + local] for k in range(0, width, local)], axis=1
    )
    gate_near = by_group(gate_near).reshape(groups, -1, local)
    early = group_scatter(jnp.concatenate([gate_near, out_near], axis=1))

    def placed(a, size):
        empty = jnp.zeros((a.shape[0], size), f32)
        return lax.dynamic_update_slice_in_dim(empty, a, chip * a.shape[1], 1)

    def tree(parts):
        while len(parts) > 1:
            parts = [a + b for a, b in zip(parts[::2], parts[1::2])]
        return parts[0]

    def small_sums(sum_channel, sum_head):
        skip = jnp.sum(sum_channel[5, :local].reshape(local_heads, HEAD), axis=1)[None]
        packed = jnp.concatenate(
            [
                jnp.concatenate(
                    [
                        placed(sum_channel[: taps + 1, :local], inner),
                        sum_channel[: taps + 1, local:],
                    ],
                    axis=1,
                ).reshape(-1),
                placed(
                    jnp.concatenate([sum_head[:2, :local_heads], skip], axis=0), heads
                ).reshape(-1),
            ]
        )
        packed = jnp.pad(packed, (0, -packed.shape[0] % 1024)).reshape(-1, LANES)
        packed = packed + sibling(packed)
        return tree([packed] + [across_chips(packed, j) for j in range(1, chips)])

    cut = (taps + 1) * (inner + 2 * N)

    def own_of(a):
        size = a.shape[1] // ranks
        return lax.dynamic_slice_in_dim(a, rank * size, size, 1)

    g_columns, sums, g_normed, far, near = [], [], [], [], []
    ready = after(by_head, gate_near, out_near, *[x for out in outs for x in out.gives])
    for b in spans:
        g_proj, sum_channel, sum_head = scan_backward(
            rank_ref, projected[b], g_results[b], g_gates[b], fronts[b][3], by_channel, ready, piece
        )
        g_columns.append(g_proj)
        sums.append((sum_channel, sum_head))
        waits = [sum_head]
        for part in outs if b == 0 else []:
            part.step(sum_head)
        if b == half - 1:
            g_proj = after(g_proj, *[x for part in g_normed for x in part.sent])
        rest = g_proj[:, local:]
        far.append(tn(normed[b][:, side:], rest))
        if b == half - 1:
            g_proj, *sums[-1] = after((g_proj, sum_channel, sum_head), early)
            rest = g_proj[:, local:]
            packed = small_sums(*[sum(part) for part in zip(*sums)])
        near.append(tn(normed[b][:, :side], rest))
        if b == 0:
            early = after(early, sum_head)
        if b == half - 1:
            rest_near = core_sum(far, near)
        send = slot_rows(g_proj, lambda x: dot_nt(x, columns))
        late = after(g_proj, rest_near) if b == half - 1 else g_proj
        keep = slot_rows(late, lambda x: dot_nt(x, columns))
        g_normed.append(Scatter(send, chips, early if b == 0 else packed, keep_rows=keep))
        if b == 0:
            if share % 16 == 0:
                gate_parts = exchanged(shares_by_chip(place, early, chips, share, local))
                early = joined_shares(
                    lambda *refs: early_kernel(width // local, *refs),
                    place,
                    [early, *gate_parts],
                    (share, 2 * inner),
                    "early_share",
                )
            else:
                gate_parts = by_chip(early[: chips * share].reshape(chips, share, local))
                out_share = jnp.split(early[chips * share :], width // local)
                out_share = jnp.concatenate(out_share, axis=1)
                early = [in_place(gate_parts, local, inner)[0]]
                early = early + jnp.split(out_share, inner // width)
                early = jnp.concatenate(early, axis=1)
            waits = [early]
            early = group_gather(early)
        ready = after(by_head, far[b], near[b], *g_normed[b].gives, *waits)
    early = after(early, rest_near)
    total_out = early[:, inner:].reshape(groups, share, -1, width)
    total_out = total_out.transpose(0, 2, 1, 3).reshape(-1, width)
    late_columns = 2 * N + LANES
    rest_blocks = by_group(rest_near).reshape(groups, -1, local + late_columns)
    if local % late_columns == 0:
        cuts = range(0, local + late_columns, late_columns)
        rest_blocks = [rest_blocks[:, :, k : k + late_columns] for k in cuts]
        rest_sum = group_scatter(jnp.concatenate(rest_blocks, axis=1))
    else:
        cuts = [0]
        rest_sum = group_scatter(rest_blocks)
    if share % 16 == 0:
        rest_parts = shares_by_chip(place, rest_sum, chips, share, local + late_columns)
        rest_total = joined_shares(
            lambda *refs: late_kernel(heads, *refs),
            place,
            exchanged(rest_parts),
            (share, inner + 2 * N + heads),
            "late_share",
        )
    else:
        rest_sum = jnp.concatenate(jnp.split(rest_sum, len(cuts)), axis=1)
        rest_parts = by_chip(rest_sum.reshape(chips, share, -1))
        shared = sum(part[:, :, local : local + 2 * N].astype(f32) for part in rest_parts)
        step_parts = [part[:, :, local + 2 * N :] for part in rest_parts]
        rest_total = jnp.concatenate(
            [
                in_place(rest_parts, local, inner),
                shared.astype(bf16),
                in_place(step_parts, local_heads, heads),
            ],
            axis=2,
        )[0]
    packed = after(packed, rest_near)
    packed = tree([packed] + [across_groups(packed, k) for k in range(1, groups)])
    packed = after(packed, rest_total).reshape(-1)
    rest_total = group_gather(rest_total)
    total_out = total_out.astype(f32)

    total_in, total_step, total_gain = weight_totals(early, rest_total, in_weight, step_weight)
    total_gain = total_gain[:, 0] / norm_gain.astype(f32)
    total_inner = jnp.sum(out_weight.astype(f32) * total_out, axis=1) / inner_gain.astype(f32)

    def regrouped(parts):
        kept = jnp.stack([part[0] for part in parts])
        got = sibling(jnp.stack([part[1] for part in parts]).astype(bf16))
        return (kept, got)

    out_sums = [out.done(rest_near) for out in outs]
    g_normed = [part.done(rest_near) for part in g_normed]

    channel_totals = own_of(packed[:cut].reshape(taps + 1, -1))
    head_totals = own_of(packed[cut : cut + 3 * heads].reshape(3, heads))

    kept, got = regrouped(out_sums)
    output = whole_call(output_kernel, core_ref, [tokens, kept, got], tokens.shape, bf16, "output")
    kept, got = regrouped(g_normed)
    token_gradient = whole_call(
        lambda *refs: token_kernel(ranks, *refs),
        core_ref,
        [tokens, cotangent, gain, kept, got],
        tokens.shape,
        f32,
        "token_gradient",
    )
    return (
        output,
        token_gradient,
        total_gain,
        total_in,
        total_step,
        channel_totals[:taps],
        channel_totals[taps],
        head_totals[0],
        head_totals[1],
        head_totals[2],
        total_inner,
        total_out,
    )


def solution(mesh):
    ranks, groups = mesh.shape["sp"], mesh.shape["dp"]
    fine = Mesh(mesh.devices.reshape(ranks // 2, 2, groups), ("chip", "core", "dp"))
    sp = ("chip", "core")
    return jax.shard_map(
        body,
        mesh=fine,
        in_specs=(
            P("dp", sp, None),
            P(sp),
            P(sp, None),
            P(sp, None),
            P(None, sp),
            P(sp),
            P(sp),
            P(sp),
            P(sp),
            P(sp),
            P(sp, None),
            P("dp", sp, None),
        ),
        out_specs=(
            P("dp", sp, None),
            P("dp", sp, None),
            P(sp),
            P(sp, None),
            P(sp, None),
            P(None, sp),
            P(sp),
            P(sp),
            P(sp),
            P(sp),
            P(sp),
            P(sp, None),
        ),
        check_vma=False,
    )
```
